128 devices in a mesh: leaf: 16 (over z, y), row: 4 (over x), col: 2 (over core).
Axes of the slice: x: 4, y: 4, z: 4, core: 2. Of those that a mesh axis runs over, the one named last changes fastest.
Arguments:
- root_inverse: float32 [16384, 16384], P('leaf', ('row', 'col')), as said below
- blocks_one: int32 [2, 16], replicated, may hold values from 0 to 127, as said below
- blocks_two: int32 [4, 16], replicated, may hold values from 0 to 23, as said below
- blocks_three: int32 [8, 16], replicated, may hold values from 0 to 23, as said below
- blocks_four: int32 [16, 16], replicated, may hold values from 0 to 23, as said below
- update_one: float32 [2048, 2048], P('col', 'leaf'), may hold values from -0.125 to 0.125
- update_two: float32 [2048, 4096], P('col', 'leaf'), may hold values from -0.125 to 0.125
- update_three: float32 [2048, 8192], P('col', 'leaf'), may hold values from -0.125 to 0.125
- update_four: float32 [2048, 16384], P('col', 'leaf'), may hold values from -0.125 to 0.125
- pivot_one: float32 [1024, 2048], P('row', 'leaf'), as said below
- pivot_two: float32 [1024, 4096], P('row', 'leaf'), as said below
- pivot_three: float32 [1024, 8192], P('row', 'leaf'), as said below
- pivot_four: float32 [1024, 16384], P('row', 'leaf'), as said below
Outputs:
- fronts_four: float32 [16, 3072, 3072], P('leaf', 'row', 'col')
The draws below stay inside these ranges and needn't reach their ends.
Inputs may be any that keep to these rules, and one draw needn't show every extreme that they name: `blocks_one`: row f lists 16 distinct root blocks; its entries of quarter p (entries p * 4 to (p + 1) * 4 - 1) are blocks of the root's quarter p, indices p * 4096 to (p + 1) * 4096 - 1. `blocks_two`: parent blocks are numbered in the parent front's order of positions, 6 blocks a quarter. The entries of quarter p of row f are the 2 separator blocks of the parent's quarter p in order, then distinct ancestor blocks of the parent's quarter p. `blocks_three`: as for blocks_two. `blocks_four`: as for blocks_two. `pivot_one`: each block of 1024 columns is symmetric. `pivot_two`: as for pivot_one. `pivot_three`: as for pivot_one. `pivot_four`: as for pivot_one. `root_inverse`: Symmetric.
All inputs are finite; a program needn't handle non-finite values.
Results may differ from the reference program's by a relative error of at most 0.0001.
Values sent between devices are 32-bit elements; how exact they have to be, the bound alone decides.
A program may use at most 192 MiB of HBM per device.

```python
import jax
import jax.numpy as jnp
from jax import lax

ROOT = 16384
SEP = 1024
ANC = 2048
BS = 128
FR = 3072


def draw_root_inverse(key, part):
    key = jax.random.fold_in(key, 11)
    base = jax.random.normal(key, (ROOT, ROOT), jnp.float32)
    diagonal = jax.random.uniform(jax.random.fold_in(key, 5), (ROOT,), jnp.float32, 1.0, 3.0)
    return (base + base.T) * 0.25 + jnp.diag(diagonal)


def pivot_draw(key, fronts):
    base = jax.random.normal(key, (fronts, SEP, SEP), jnp.float32) * 0.2
    diagonal = jax.random.uniform(jax.random.fold_in(key, 5), (fronts, SEP), jnp.float32, 1.0, 2.0)
    full = base + jnp.swapaxes(base, 1, 2) + diagonal[:, :, None] * jnp.eye(SEP, dtype=jnp.float32)[None]
    return jnp.transpose(full, (1, 0, 2)).reshape(SEP, fronts * SEP)


def draw_pivot_one(key, part):
    key = jax.random.fold_in(key, 21)
    return pivot_draw(key, 2)


def draw_pivot_two(key, part):
    key = jax.random.fold_in(key, 22)
    return pivot_draw(key, 4)


def draw_pivot_three(key, part):
    key = jax.random.fold_in(key, 23)
    return pivot_draw(key, 8)


def draw_pivot_four(key, part):
    key = jax.random.fold_in(key, 24)
    return pivot_draw(key, 16)


def draw_blocks_one(key, part):
    key = jax.random.fold_in(key, 31)
    per_quarter = ROOT // BS // 4
    taken = ANC // BS // 4
    keys = jax.random.split(key, 8)
    picks = jax.vmap(lambda single: jax.random.permutation(single, per_quarter)[:taken])(keys)
    offsets = jnp.arange(8, dtype=jnp.int32) % 4 * per_quarter
    return (picks.astype(jnp.int32) + offsets[:, None]).reshape(2, 4 * taken)


def child_blocks(key, fronts):
    sep_part = SEP // BS // 4
    anc_part = ANC // BS // 4
    quarter_blocks = sep_part + anc_part
    keys = jax.random.split(key, fronts * 4)
    picks = jax.vmap(lambda single: jax.random.permutation(single, anc_part)[:anc_part - sep_part])(keys)
    quarter = jnp.arange(fronts * 4, dtype=jnp.int32) % 4
    leading = quarter[:, None] * quarter_blocks + jnp.arange(sep_part, dtype=jnp.int32)[None, :]
    chosen = quarter[:, None] * quarter_blocks + sep_part + picks.astype(jnp.int32)
    return jnp.concatenate([leading, chosen], 1).reshape(fronts, 4 * anc_part)


def draw_blocks_two(key, part):
    key = jax.random.fold_in(key, 32)
    return child_blocks(key, 4)


def draw_blocks_three(key, part):
    key = jax.random.fold_in(key, 33)
    return child_blocks(key, 8)


def draw_blocks_four(key, part):
    key = jax.random.fold_in(key, 34)
    return child_blocks(key, 16)


def steps_of(stream_key, extent, cuts, smallest, largest):
    def one(position, shards_of):
        heights = jax.random.uniform(jax.random.fold_in(jax.random.fold_in(stream_key, 6), position), (shards_of,), jnp.float32, smallest / len(cuts), largest / len(cuts))
        return jnp.repeat(jnp.exp(heights), extent[position] // shards_of).reshape((-1,) + (1,) * (len(extent) - position - 1))

    gain = one(*cuts[0])
    for cut in cuts[1:]:
        gain = gain * one(*cut)
    return gain


def bell_draw(stream_key, shape, scale, reach, pieces=(), kind=jnp.bfloat16):
    entries = jax.random.normal(stream_key, shape, jnp.float32) * scale
    if len(pieces) > 0:
        entries = steps_of(stream_key, shape, pieces, -0.22, 0.18) * entries
    return jnp.clip(entries, min=-reach, max=reach).astype(kind)


def setup_inputs(seed: int = 0) -> dict:
    seeds = jax.random.split(jax.random.key(seed), 14)
    return {
        "root_inverse": draw_root_inverse(jax.random.fold_in(seeds[13], 71), 0),
        "blocks_one": draw_blocks_one(jax.random.fold_in(seeds[13], 71), 0),
        "blocks_two": draw_blocks_two(jax.random.fold_in(seeds[13], 71), 0),
        "blocks_three": draw_blocks_three(jax.random.fold_in(seeds[13], 71), 0),
        "blocks_four": draw_blocks_four(jax.random.fold_in(seeds[13], 71), 0),
        "update_one": bell_draw(seeds[5], (ANC, 2 * SEP), ANC ** -0.5, 0.125, ((0, 2), (1, 16)), jnp.float32),
        "update_two": bell_draw(seeds[6], (ANC, 4 * SEP), ANC ** -0.5, 0.125, ((0, 2), (1, 16)), jnp.float32),
        "update_three": bell_draw(seeds[7], (ANC, 8 * SEP), ANC ** -0.5, 0.125, ((0, 2), (1, 16)), jnp.float32),
        "update_four": bell_draw(seeds[8], (ANC, 16 * SEP), ANC ** -0.5, 0.125, ((0, 2), (1, 16)), jnp.float32),
        "pivot_one": draw_pivot_one(jax.random.fold_in(seeds[13], 71), 0),
        "pivot_two": draw_pivot_two(jax.random.fold_in(seeds[13], 71), 0),
        "pivot_three": draw_pivot_three(jax.random.fold_in(seeds[13], 71), 0),
        "pivot_four": draw_pivot_four(jax.random.fold_in(seeds[13], 71), 0),
    }


HIGH = lax.Precision.HIGHEST


def expand(ids):
    offsets = jnp.arange(BS, dtype=jnp.int32)
    return (ids.astype(jnp.int32)[:, None] * BS + offsets[None, :]).reshape(-1)


def build_front(square, panel, held):
    sep_q = SEP // 4
    anc_q = ANC // 4
    sep_sep = square.reshape(4, sep_q, 4, sep_q)
    sep_anc = (-panel.T).reshape(4, sep_q, 4, anc_q)
    anc_sep = (-panel).reshape(4, anc_q, 4, sep_q)
    anc_anc = held.reshape(4, anc_q, 4, anc_q)
    top = jnp.concatenate([sep_sep, sep_anc], 3)
    bottom = jnp.concatenate([anc_sep, anc_anc], 3)
    return jnp.concatenate([top, bottom], 1).reshape(FR, FR)


def solve_front(held, update, pivot):
    panel = jnp.dot(held, update, precision=HIGH, preferred_element_type=jnp.float32)
    square = pivot + jnp.dot(panel.T, update, precision=HIGH, preferred_element_type=jnp.float32)
    return build_front(square, panel, held)


def reference(root_inverse, blocks_one, blocks_two, blocks_three, blocks_four, update_one, update_two, update_three, update_four, pivot_one, pivot_two, pivot_three, pivot_four):
    updates = (update_two, update_three, update_four)
    pivots = (pivot_two, pivot_three, pivot_four)
    lists = (blocks_two, blocks_three, blocks_four)
    fronts = []
    for front in range(2):
        index = expand(blocks_one[front])
        held = jnp.take(jnp.take(root_inverse, index, axis=0), index, axis=1)
        fronts.append(solve_front(held, update_one[:, front * SEP:(front + 1) * SEP], pivot_one[:, front * SEP:(front + 1) * SEP]))
    for depth in range(3):
        children = []
        for front in range(2 ** (depth + 2)):
            index = expand(lists[depth][front])
            held = jnp.take(jnp.take(fronts[front // 2], index, axis=0), index, axis=1)
            children.append(solve_front(held, updates[depth][:, front * SEP:(front + 1) * SEP], pivots[depth][:, front * SEP:(front + 1) * SEP]))
        fronts = children
    return jnp.stack(fronts)
```

```python
import functools

import jax
import jax.numpy as jnp
from jax import lax
from jax.experimental import pallas as pl
from jax.experimental.pallas import tpu as pltpu
from jax.sharding import Mesh, PartitionSpec as P

SEP = 1024
ANC = 2048
BS = 128
AXES = ("za", "zb", "ya", "yb", "row", "col")
MESH = pl.DeviceIdType.MESH
VMEM = pl.BlockSpec(memory_space=pltpu.VMEM)
SMEM = pl.BlockSpec(memory_space=pltpu.SMEM)
ANY = pl.BlockSpec(memory_space=pl.ANY)
F32 = jnp.float32
BF16 = jnp.bfloat16


def place():
    z = lax.axis_index("za") * 2 + lax.axis_index("zb")
    y = lax.axis_index("ya") * 2 + lax.axis_index("yb")
    return z, y, lax.axis_index("row"), lax.axis_index("col")


def device(z, y, x, c):
    return (z // 2, z % 2, y // 2, y % 2, x, c)


def halves(value):
    high = value.astype(BF16)
    return high, (value - high.astype(F32)).astype(BF16)


def dot(a, b):
    return jnp.dot(a, b, preferred_element_type=F32)


def pick_kernel(ids_ref, root_ref, out_ref, blocks, sems):
    z, y, x, c = place()

    def source(f, j, i):
        row = ids_ref[f, z * 4 + i] - (z * 4 + y) * 8
        col = ids_ref[f, x * 4 + j] - (x * 2 + c) * 16
        valid = (row >= 0) & (row < 8) & (col >= 0) & (col < 16)
        return jnp.clip(row, 0, 7), jnp.clip(col, 0, 15), valid

    def copy(n, row, col):
        return pltpu.make_async_copy(
            root_ref.at[
                pl.ds(pl.multiple_of(row * BS, BS), BS), pl.ds(pl.multiple_of(col * BS, BS), BS)
            ],
            blocks.at[n],
            sems.at[n],
        )

    triples = [(f, j, i) for f in range(2) for j in range(4) for i in range(4)]
    for n, (f, j, i) in enumerate(triples):
        row, col, _ = source(f, j, i)
        copy(n, row, col).start()
    for n, (f, j, i) in enumerate(triples):
        row, col, valid = source(f, j, i)
        copy(n, row, col).wait()
        at = i % 2 * 2 + i // 2
        out_ref[f, j, at] = jnp.where(valid, blocks[n].T, 0.0)


def pick(ids, root):
    return pl.pallas_call(
        pick_kernel,
        out_shape=jax.ShapeDtypeStruct((2, 4, 4, BS, BS), F32),
        in_specs=[SMEM, ANY],
        out_specs=VMEM,
        scratch_shapes=[pltpu.VMEM((32, BS, BS), F32), pltpu.SemaphoreType.DMA((32,))],
        compiler_params=pltpu.CompilerParams(vmem_limit_bytes=32 * 2**20),
        name="pick",
    )(ids, root)


def spread_kernel(m_ref, out_ref, core_in, mine, y_in, ready, core_s, core_r, ys, yr, hs, hr):
    z, y, x, c = place()
    barrier = pltpu.get_barrier_semaphore()

    def signal(dev):
        pl.semaphore_signal(barrier, inc=1, device_id=dev, device_id_type=MESH)

    mine_f = z // 2
    signal(device(z, y, x, 1 - c))
    for d in range(1, 4):
        signal(device(z, (y + d) % 4, x, c))
    for p in range(4):
        for r in range(2):
            j = 2 * r + c

            @pl.when(jnp.logical_not((p == z) & (j == y) & (mine_f == c)))
            def _():
                signal(device(p, j, x, mine_f))

    own = (mine_f == c) & (y % 2 == c)
    pl.semaphore_wait(barrier, jnp.where(own, 11, 12))

    core = pltpu.make_async_remote_copy(
        src_ref=m_ref.at[1 - c],
        dst_ref=core_in,
        send_sem=core_s,
        recv_sem=core_r,
        device_id=device(z, y, x, 1 - c),
        device_id_type=MESH,
    )
    core.start()
    core.wait()
    mine[...] = m_ref[c] + core_in[...]

    def y_copy(d):
        to = (y + d) % 4
        return pltpu.make_async_remote_copy(
            src_ref=mine.at[to],
            dst_ref=y_in.at[d - 1],
            send_sem=ys.at[d - 1],
            recv_sem=yr.at[d - 1],
            device_id=device(z, to, x, c),
            device_id_type=MESH,
        )

    for d in (2, 1, 3):
        y_copy(d).start()
    for d in (1, 3, 2):
        y_copy(d).wait()
    ready[...] = mine[y] + y_in[0] + y_in[1] + y_in[2]

    def h_copy(k, d):
        return pltpu.make_async_remote_copy(
            src_ref=ready,
            dst_ref=out_ref.at[y // 2, pl.ds(4 * z, 4)],
            send_sem=hs.at[k * 4 + d],
            recv_sem=hr.at[z * 2 + y // 2],
            device_id=device(2 * c + k, (y + d) % 4, x, y % 2),
            device_id_type=MESH,
        )

    def to_self(k, d):
        return (2 * c + k == z) & (d == 0) & (y % 2 == c)

    for d in (2, 1, 3, 0):
        for k in range(2):
            if d == 0:

                @pl.when(jnp.logical_not(to_self(k, d)))
                def _():
                    h_copy(k, d).start()

                @pl.when(to_self(k, d))
                def _():
                    out_ref[y // 2, pl.ds(4 * z, 4)] = ready[...]

            else:
                h_copy(k, d).start()
    for d in (2, 1, 3, 0):
        for k in range(2):
            if d == 0:

                @pl.when(jnp.logical_not(to_self(k, d)))
                def _():
                    h_copy(k, d).wait_send()

            else:
                h_copy(k, d).wait_send()
    for p in range(4):
        for r in range(2):

            @pl.when(jnp.logical_not((p == z) & (2 * r + c == y) & (mine_f == c)))
            def _():
                pltpu.make_async_remote_copy(
                    src_ref=ready,
                    dst_ref=out_ref.at[r, pl.ds(4 * p, 4)],
                    send_sem=hs.at[0],
                    recv_sem=hr.at[p * 2 + r],
                    device_id=device(z, y, x, 1 - c),
                    device_id_type=MESH,
                ).wait_recv()


def spread(picked):
    return pl.pallas_call(
        spread_kernel,
        out_shape=jax.ShapeDtypeStruct((2, 16, BS, BS), F32),
        in_specs=[VMEM],
        out_specs=VMEM,
        scratch_shapes=[
            pltpu.VMEM((4, 4, BS, BS), F32),
            pltpu.VMEM((4, 4, BS, BS), F32),
            pltpu.VMEM((3, 4, BS, BS), F32),
            pltpu.VMEM((4, BS, BS), F32),
            pltpu.SemaphoreType.DMA,
            pltpu.SemaphoreType.DMA,
            pltpu.SemaphoreType.DMA((3,)),
            pltpu.SemaphoreType.DMA((3,)),
            pltpu.SemaphoreType.DMA((8,)),
            pltpu.SemaphoreType.DMA((8,)),
        ],
        compiler_params=pltpu.CompilerParams(
            collective_id=0, has_side_effects=True, vmem_limit_bytes=48 * 2**20
        ),
        name="spread",
    )(picked)


def level_kernel(
    last, sel_ref, h_ref, u_ref, v_ref, out_ref,
    hq, pq, uhi, ulo, hs, st, ptl, acc, xin, xs_s, xs_r, ss, rs, hx_s, hx_r, px_s, px_r,
):
    z, y, q, c = place()
    e = 2 * q + c
    partner = device(z, y, q, 1 - c)
    barrier = pltpu.get_barrier_semaphore()
    for t in range(8):

        @pl.when(t != e)
        def _():
            pl.semaphore_signal(
                barrier, inc=1, device_id=device(z, y, t // 2, t % 2), device_id_type=MESH
            )

    def split_u(b, carry):
        m = b // 2
        src = 4 * (m // 2) + 2 * (b % 2) + m % 2
        hi, lo = halves(u_ref[pl.ds(pl.multiple_of(src * BS, BS), BS), :])
        at = pl.ds(pl.multiple_of(b * BS, BS), BS)
        uhi[at, :] = hi
        ulo[at, :] = lo
        return carry

    lax.fori_loop(0, 16, split_u, 0)
    for r in range(2):
        for b in range(16):
            value = h_ref[r, b]
            hi, lo = halves(value)
            hs[r * BS : r * BS + BS, b * BS : b * BS + BS] = hi
            hs[256 + r * BS : 256 + r * BS + BS, b * BS : b * BS + BS] = lo
            hq[2 * r + c, b] = value
    pl.semaphore_wait(barrier, 7)

    def core_copy(ref, r, s_sem, r_sem):
        return pltpu.make_async_remote_copy(
            src_ref=ref.at[2 * r + c],
            dst_ref=ref.at[2 * r + c],
            send_sem=s_sem.at[r],
            recv_sem=r_sem.at[r],
            device_id=partner,
            device_id_type=MESH,
        )

    def core_arrived(ref, r, s_sem, r_sem):
        return pltpu.make_async_remote_copy(
            src_ref=ref.at[2 * r + 1 - c],
            dst_ref=ref.at[2 * r + 1 - c],
            send_sem=s_sem.at[r],
            recv_sem=r_sem.at[r],
            device_id=partner,
            device_id_type=MESH,
        )

    for r in range(2):
        core_copy(hq, r, hx_s, hx_r).start()

    def piece(to):
        return pltpu.make_async_remote_copy(
            src_ref=st.at[to],
            dst_ref=ptl.at[pl.ds(2 * e, 2)],
            send_sem=ss.at[to],
            recv_sem=rs.at[e],
            device_id=device(z, y, to // 2, to % 2),
            device_id_type=MESH,
        )

    def panel_step(k, carry):
        t = lax.rem(q + jnp.where(k == 0, 2, jnp.where(k == 1, 1, jnp.where(k == 2, 3, 0))), 4)
        cols = pl.ds(pl.multiple_of(t * 256, 256), 256)
        both = dot(hs[...], uhi[:, cols])
        part = both[:256] + both[256:] + dot(hs[:256, :], ulo[:, cols])
        for r in range(2):
            pq[2 * r + c, :, cols] = part[r * BS : r * BS + BS]
        for core in range(2):
            to = 2 * t + core
            turned = [part[r * BS : r * BS + BS, core * BS : core * BS + BS].T for r in range(2)]

            @pl.when(to == e)
            def _():
                for r in range(2):
                    ptl[2 * e + r] = turned[r]

            @pl.when(to != e)
            def _():
                for r in range(2):
                    st[to, r] = turned[r]
                piece(to).start()

        return carry

    lax.fori_loop(0, 4, panel_step, 0)
    for r in range(2):
        core_copy(pq, r, px_s, px_r).start()
    acc[...] = v_ref[...]

    def square_step(s, carry):
        k = s // 2
        t = lax.rem(q + jnp.where(k == 0, 0, jnp.where(k == 1, 1, jnp.where(k == 2, 3, 2))), 4)
        m = 2 * t + lax.rem(s + c, 2)

        @pl.when(m != e)
        def _():
            pltpu.make_async_remote_copy(
                src_ref=st.at[m],
                dst_ref=ptl.at[pl.ds(2 * m, 2)],
                send_sem=ss.at[m],
                recv_sem=rs.at[m],
                device_id=partner,
                device_id_type=MESH,
            ).wait_recv()

        hi, lo = halves(jnp.concatenate([ptl[2 * m], ptl[2 * m + 1]], 1))
        rows = pl.ds(pl.multiple_of(m * 256, 256), 256)
        both = dot(jnp.concatenate([hi, lo], 0), uhi[rows, :])
        acc[...] += both[:BS] + both[BS:] + dot(hi, ulo[rows, :])
        return carry

    lax.fori_loop(0, 8, square_step, 0)

    for r in range(2):
        core_arrived(hq, r, hx_s, hx_r).wait_recv()
        core_arrived(pq, r, px_s, px_r).wait_recv()

    if not last:
        mine = sel_ref[0, e]
        for m in range(8):
            block = sel_ref[1, m]
            out_ref[0, 2 * m] = acc[:, m * BS : m * BS + BS]
            out_ref[0, 2 * m + 1] = -ptl[block]
            out_ref[1, 2 * m] = -pq[mine, :, m * BS : m * BS + BS]
            out_ref[1, 2 * m + 1] = hq[mine, block]
    else:
        def rows_of(half):
            for p in range(2):
                quarter = 2 * half + p
                yield p * 768, acc[:, pl.ds(pl.multiple_of(quarter * 256, 256), 256)]
                for a in range(4):
                    yield p * 768 + 256 + a * BS, -ptl[2 * (2 * quarter + a % 2) + a // 2]

        for at, value in rows_of(1 - c):
            xin[1, :, at : at + value.shape[1]] = value
        cross = pltpu.make_async_remote_copy(
            src_ref=xin.at[1],
            dst_ref=xin.at[0],
            send_sem=xs_s,
            recv_sem=xs_r,
            device_id=partner,
            device_id_type=MESH,
        )
        cross.start()
        mine_at = pl.ds(pl.multiple_of(c * BS, BS), BS)
        for at, value in rows_of(c):
            out_ref[0, mine_at, at : at + value.shape[1]] = value
        for a in range(4):
            rows = slice(256 + a * BS, 256 + a * BS + BS)
            for p in range(2):
                quarter = 2 * c + p
                cols = pl.ds(pl.multiple_of(quarter * 256, 256), 256)
                out_ref[0, rows, p * 768 : p * 768 + 256] = -pq[a, :, cols]
                for b in range(4):
                    block = 2 * (2 * quarter + b % 2) + b // 2
                    to = p * 768 + 256 + b * BS
                    out_ref[0, rows, to : to + BS] = hq[a, block]
        cross.wait()
        out_ref[0, pl.ds(pl.multiple_of((1 - c) * BS, BS), BS), :] = xin[0]

    for r in range(2):
        core_copy(hq, r, hx_s, hx_r).wait_send()
        core_copy(pq, r, px_s, px_r).wait_send()

    def sent(to, carry):
        @pl.when(to != e)
        def _():
            piece(to).wait_send()

        return carry

    lax.fori_loop(0, 8, sent, 0)


def level(depth, sel, held, update, pivot):
    last = depth == 3
    shape = (1, 768, 1536) if last else (2, 16, BS, BS)
    sem = pltpu.SemaphoreType.DMA
    return pl.pallas_call(
        functools.partial(level_kernel, last),
        out_shape=jax.ShapeDtypeStruct(shape, F32),
        in_specs=[SMEM, VMEM, VMEM, VMEM],
        out_specs=VMEM,
        scratch_shapes=[
            pltpu.VMEM((4, 16, BS, BS), F32),
            pltpu.VMEM((4, BS, SEP), F32),
            pltpu.VMEM((ANC, SEP), BF16),
            pltpu.VMEM((ANC, SEP), BF16),
            pltpu.VMEM((512, ANC), BF16),
            pltpu.VMEM((8, 2, BS, BS), F32),
            pltpu.VMEM((16, BS, BS), F32),
            pltpu.VMEM((BS, SEP), F32),
            pltpu.VMEM((2, BS, 1536), F32),
            sem,
            sem,
            sem((8,)),
            sem((8,)),
            sem((2,)),
            sem((2,)),
            sem((2,)),
            sem((2,)),
        ],
        compiler_params=pltpu.CompilerParams(
            collective_id=1 + depth, has_side_effects=True, vmem_limit_bytes=56 * 2**20
        ),
        name="level_%d" % (depth + 1),
    )(sel, held, update, pivot)


def shards(
    root_inverse,
    blocks_one,
    blocks_two,
    blocks_three,
    blocks_four,
    update_one,
    update_two,
    update_three,
    update_four,
    pivot_one,
    pivot_two,
    pivot_three,
    pivot_four,
):
    z, y, _, c = place()
    leaf = z * 4 + y
    groups = (("zb", "ya", "yb"), ("ya", "yb"), ("yb",), ())
    updates = (update_one, update_two, update_three, update_four)
    pivots = (pivot_one, pivot_two, pivot_three, pivot_four)
    lists = (blocks_two, blocks_three, blocks_four, blocks_four)
    full, rows = [], []
    for axes, update, pivot in zip(groups, updates, pivots):
        value = lax.dynamic_slice_in_dim(pivot, c * BS, BS, 0)
        if axes:
            update = lax.all_gather(update, axes, axis=1, tiled=True)
            value = lax.all_gather(value, axes, axis=1, tiled=True)
        full.append(lax.all_gather(update, "col", axis=0, tiled=True))
        rows.append(value)
    held = spread(pick(blocks_one, root_inverse))
    for depth in range(4):
        ids = lax.dynamic_index_in_dim(
            lists[depth], leaf // max(1, 4 >> depth), 0, keepdims=False
        )
        listed = ids.reshape(4, 4)[:, 2:] - 6 * jnp.arange(4, dtype=jnp.int32)[:, None] - 2
        chosen = jnp.clip(listed.reshape(8), 0, 3)
        quarters = jnp.arange(8, dtype=jnp.int32) // 2
        sel = jnp.stack([chosen, 4 * quarters + 2 * (chosen % 2) + chosen // 2])
        held = level(depth, sel, held, full[depth], rows[depth])
    return held


def solution(mesh):
    mesh = Mesh(mesh.devices.reshape(2, 2, 2, 2, 4, 2), AXES)
    leaf = AXES[:4]
    placed = (
        P(leaf, ("row", "col")),
        P(),
        P(),
        P(),
        P(),
        P("col", leaf),
        P("col", leaf),
        P("col", leaf),
        P("col", leaf),
        P("row", leaf),
        P("row", leaf),
        P("row", leaf),
        P("row", leaf),
    )
    return jax.shard_map(
        shards, mesh=mesh, in_specs=placed, out_specs=P(leaf, "row", "col"), check_vma=False
    )
```

```python
import jax
import jax.numpy as jnp
from jax import lax
from jax.experimental import pallas as pl
from jax.experimental.pallas import tpu as pltpu
from jax.sharding import Mesh, PartitionSpec as P

SEP = 1024
ANC = 2048
BS = 128
UNIT = 256
AXES = ("za", "zb", "ya", "yb", "row", "col")
MESH = pl.DeviceIdType.MESH
F32 = jnp.float32
BF16 = jnp.bfloat16
SHARE = (4, 2, 2)


def place():
    z = lax.axis_index("za") * 2 + lax.axis_index("zb")
    y = lax.axis_index("ya") * 2 + lax.axis_index("yb")
    return z, y, lax.axis_index("row"), lax.axis_index("col")


def device(z, y, x, c):
    return (z // 2, z % 2, y // 2, y % 2, x, c)


def halves(value):
    high = value.astype(BF16)
    return high, (value - high.astype(F32)).astype(BF16)


def dot(a, b):
    return jnp.dot(a, b, preferred_element_type=F32)


def block_at(index, size):
    return pl.ds(pl.multiple_of(index * size, size), size)


def remote(src, dst, send, recv, to):
    return pltpu.make_async_remote_copy(
        src_ref=src, dst_ref=dst, send_sem=send, recv_sem=recv, device_id=to, device_id_type=MESH
    )


class Gather:
    def __init__(self, level, spot, u, v, ug, vg, sems):
        self.level, self.u, self.v, self.ug, self.vg = level, u, v, ug, vg
        self.z, self.y, self.x, self.c = spot
        self.own_sem, self.a_s, self.a_r, self.b_s, self.b_r, self.c_s, self.c_r, self.v_s, self.v_r = sems
        self.count = 8 >> level
        self.width = SEP // self.count
        self.share = SHARE[level]
        self.me = lax.rem(self.z * 4 + self.y, self.count)
        self.first = self.x if self.share == 4 else 2 * lax.rem(self.x, 2)
        self.units = 4 // self.share
        if self.share == 4:
            self.hops = ((1, 0, 1), (3, 0, 1), (2, 0, 1))
        else:
            self.hops = ((1, 0, 1), (3, 1, 1))

    def peer(self, d):
        base = (self.z * 4 + self.y) // self.count * self.count
        return lax.rem(self.me + d, self.count), base

    def leaf(self, member, base):
        at = base + member
        return device(at // 4, lax.rem(at, 4), self.x, self.c)

    def cols(self, member):
        return block_at(member, self.width)

    def rows(self, first, units):
        return pl.ds(pl.multiple_of(first * UNIT, UNIT), units * UNIT)

    def own(self):
        return (
            pltpu.make_async_copy(self.u, self.ug.at[self.c, :, self.cols(self.me)], self.own_sem.at[0]),
            pltpu.make_async_copy(
                self.v.at[block_at(self.c, BS), :], self.vg.at[:, self.cols(self.me)], self.own_sem.at[1]
            ),
        )

    def a_copy(self, d):
        member, base = self.peer(d)
        rows = self.rows(self.first, self.units)
        return remote(
            self.u.at[rows, :], self.ug.at[self.c, rows, self.cols(self.me)],
            self.a_s.at[d], self.a_r.at[self.me], self.leaf(member, base),
        )

    def v_copy(self, d):
        member, base = self.peer(d)
        return remote(
            self.v.at[block_at(self.c, BS), :], self.vg.at[:, self.cols(self.me)],
            self.v_s.at[d], self.v_r.at[self.me], self.leaf(member, base),
        )

    def a_arrived(self, member):
        rows = self.rows(self.first, self.units)
        there = self.ug.at[self.c, rows, self.cols(member)]
        return remote(there, there, self.a_s.at[0], self.a_r.at[member], device(self.z, self.y, self.x, 1 - self.c))

    def v_arrived(self, member):
        there = self.vg.at[:, self.cols(member)]
        return remote(there, there, self.v_s.at[0], self.v_r.at[member], device(self.z, self.y, self.x, 1 - self.c))

    def b_copy(self, n, member):
        step, first, units = self.hops[n]
        there = self.ug.at[self.c, self.rows(self.first + first, units), self.cols(member)]
        to = device(self.z, self.y, lax.rem(self.x + step, 4), self.c)
        return remote(there, there, self.b_s.at[n, member], self.b_r.at[n, member], to)

    def b_arrived(self, n, member):
        step, first, units = self.hops[n]
        source = lax.rem(self.x + 4 - step, 4)
        start = source if self.share == 4 else 2 * lax.rem(source, 2)
        there = self.ug.at[self.c, self.rows(start + first, units), self.cols(member)]
        return remote(
            there, there, self.b_s.at[n, member], self.b_r.at[n, member],
            device(self.z, self.y, self.x, 1 - self.c),
        )

    def c_copy(self, unit, half):
        there = self.ug.at[half, self.rows(unit, 1), :]
        return remote(
            there, there, self.c_s.at[unit], self.c_r.at[unit], device(self.z, self.y, self.x, 1 - self.c)
        )

    def unit(self, n):
        return lax.rem(self.first + n, 4)

    def begin(self):
        for copy in self.own():
            copy.start()

    def send(self):
        for d in range(1, self.count):
            self.a_copy(d).start()
            self.v_copy(d).start()

    def share_out(self):
        for copy in self.own():
            copy.wait()

        def step(d, carry):
            member = lax.rem(self.me + self.count - d, self.count)
            self.a_arrived(member).wait_recv()
            for n in range(len(self.hops)):
                self.b_copy(n, member).start()
            return carry

        lax.fori_loop(1, self.count, step, 0)
        for n in range(self.units):
            self.c_copy(self.unit(n), self.c).start()

    def collect(self):
        def step(d, carry):
            member = lax.rem(self.me + self.count - d, self.count)
            for n in range(len(self.hops)):
                self.b_arrived(n, member).wait_recv()
            self.v_arrived(member).wait_recv()
            return carry

        lax.fori_loop(1, self.count, step, 0)
        for n in range(self.units, 4):
            self.c_copy(self.unit(n), self.c).start()

    def wait_other(self, unit):
        self.c_copy(unit, 1 - self.c).wait_recv()

    def finish(self):
        def step(d, carry):
            self.a_copy(d).wait_send()
            self.v_copy(d).wait_send()
            member = lax.rem(self.me + self.count - d, self.count)
            for n in range(len(self.hops)):
                self.b_copy(n, member).wait_send()
            return carry

        lax.fori_loop(1, self.count, step, 0)
        for unit in range(4):
            self.c_copy(unit, self.c).wait_send()


def whole_kernel(
    tab_ref, mask_ref, sel_ref, root_ref, u1, u2, u3, u4, v1, v2, v3, v4,
    out_ref, ug1, ug2, ug3, ug4,
    rootv, picked, core_in, mine, y_in, ready, held, hq0, hq1, pq0, pq1, ptl0, ptl1, uhi, ulo, stage, hs, st, vg, acc, xin,
    root_sem, core_s, core_r, ys, yr, h_s, h_r,
    own1, a1s, a1r, b1s, b1r, c1s, c1r, w1s, w1r,
    own2, a2s, a2r, b2s, b2r, c2s, c2r, w2s, w2r,
    own3, a3s, a3r, b3s, b3r, c3s, c3r, w3s, w3r,
    c4s, c4r, v4_sem, stage_sem, ps, pr, hx_s, hx_r, px_s, px_r, xs_s, xs_r,
):
    spot = place()
    z, y, q, c = spot
    e = 2 * q + c
    partner = device(z, y, q, 1 - c)
    g1 = Gather(0, spot, u1, v1, ug1, vg.at[0], (own1, a1s, a1r, b1s, b1r, c1s, c1r, w1s, w1r))
    g2 = Gather(1, spot, u2, v2, ug2, vg.at[1], (own2, a2s, a2r, b2s, b2r, c2s, c2r, w2s, w2r))
    g3 = Gather(2, spot, u3, v3, ug3, vg.at[2], (own3, a3s, a3r, b3s, b3r, c3s, c3r, w3s, w3r))
    gathers = (g1, g2, g3)

    barrier = pltpu.get_barrier_semaphore()

    def signal(dev):
        pl.semaphore_signal(barrier, inc=1, device_id=dev, device_id_type=MESH)

    mine_f = z // 2

    def root_copy(j):
        return pltpu.make_async_copy(
            root_ref.at[:, :, j * BS : j * BS + BS], rootv.at[j], root_sem.at[j]
        )

    for j in range(16):
        root_copy(j).start()
    for g in gathers:
        g.begin()
    for t in range(8):

        @pl.when(t != e)
        def _():
            signal(device(z, y, t // 2, t % 2))

    for d in range(1, 8):
        member, base = g1.peer(d)
        signal(g1.leaf(member, base))
    for p in range(4):
        for r in range(2):
            j = 2 * r + c

            @pl.when(jnp.logical_not((p == z) & (j == y) & (mine_f == c)))
            def _():
                signal(device(p, j, q, mine_f))

    own = (mine_f == c) & (y % 2 == c)
    pl.semaphore_wait(barrier, jnp.where(own, 21, 22))

    g1.send()

    def u4_push(unit):
        rows = pl.ds(unit * UNIT, UNIT)
        return remote(u4.at[rows, :], ug4.at[rows, :], c4s.at[unit], c4r.at[unit], partner)

    def v4_copy():
        return pltpu.make_async_copy(v4.at[block_at(c, BS), :], acc.at[1], v4_sem)

    for unit in range(4):
        u4_push(unit).start()
    v4_copy().start()

    for j in range(16):
        root_copy(j).wait()

    def pick(n, carry):
        f, j = n // 4, n % 4
        for i in range(4):
            at = n * 4 + i
            block = rootv[tab_ref[32 + at], tab_ref[at]]
            picked[f, j, i % 2 * 2 + i // 2] = (block * mask_ref[at]).T
        return carry

    lax.fori_loop(0, 8, pick, 0)
    core = remote(picked.at[1 - c], core_in, core_s, core_r, partner)
    core.start()
    core.wait()
    mine[...] = picked[c] + core_in[...]

    def y_copy(d):
        to = lax.rem(y + d, 4)
        return remote(mine.at[to], y_in.at[d - 1], ys.at[d - 1], yr.at[d - 1], device(z, to, q, c))

    for d in (2, 1, 3):
        y_copy(d).start()
    for d in (1, 3, 2):
        y_copy(d).wait()
    ready[...] = mine[y] + y_in[0] + y_in[1] + y_in[2]

    def h_copy(k, d):
        return remote(
            ready, held.at[y // 2, pl.ds(4 * z, 4)], h_s.at[k * 4 + d], h_r.at[z * 2 + y // 2],
            device(2 * c + k, lax.rem(y + d, 4), q, y % 2),
        )

    def to_self(k):
        return (2 * c + k == z) & (y % 2 == c)

    for d in (2, 1, 3):
        for k in range(2):
            h_copy(k, d).start()
    for k in range(2):

        @pl.when(jnp.logical_not(to_self(k)))
        def _():
            h_copy(k, 0).start()

        @pl.when(to_self(k))
        def _():
            held[y // 2, pl.ds(4 * z, 4)] = ready[...]

    g1.share_out()
    for p in range(4):
        for r in range(2):

            @pl.when(jnp.logical_not((p == z) & (2 * r + c == y) & (mine_f == c)))
            def _():
                there = held.at[r, pl.ds(4 * p, 4)]
                remote(there, there, h_s.at[0], h_r.at[p * 2 + r], partner).wait_recv()

    g2.send()
    for d in (2, 1, 3):
        for k in range(2):
            h_copy(k, d).wait_send()
    for k in range(2):

        @pl.when(jnp.logical_not(to_self(k)))
        def _():
            h_copy(k, 0).wait_send()

    def pair_copy(ref, at, r, s_sem, r_sem):
        return remote(
            ref.at[2 * r + c], ref.at[2 * r + c], s_sem.at[at, r], r_sem.at[at, r], partner
        )

    def pair_arrived(ref, at, r, s_sem, r_sem):
        there = ref.at[2 * r + 1 - c]
        return remote(there, there, s_sem.at[at, r], r_sem.at[at, r], partner)

    def split_update(depth):
        def unit_of(n):
            first = gathers[depth].first if depth < 3 else 0
            return lax.rem(first + n // 2, 4), lax.rem(n + c, 2)

        def fetch(n, slot):
            unit, half = unit_of(n)
            rows = pl.ds(pl.multiple_of(unit * UNIT, UNIT), UNIT)
            if depth < 3:
                pltpu.make_async_copy(
                    gathers[depth].ug.at[half, rows, :], stage.at[slot], stage_sem.at[slot]
                ).start()
            else:

                @pl.when(half == c)
                def _():
                    pltpu.make_async_copy(u4.at[rows, :], stage.at[slot], stage_sem.at[slot]).start()

                @pl.when(half != c)
                def _():
                    pltpu.make_async_copy(ug4.at[rows, :], stage.at[slot], stage_sem.at[slot]).start()

        def arrived(n):
            unit, half = unit_of(n)

            @pl.when(half != c)
            def _():
                if depth < 3:
                    gathers[depth].wait_other(unit)
                else:
                    rows = pl.ds(pl.multiple_of(unit * UNIT, UNIT), UNIT)
                    remote(
                        ug4.at[rows, :], ug4.at[rows, :], c4s.at[unit], c4r.at[unit], partner
                    ).wait_recv()

        def step(n, carry):
            slot = lax.rem(n, 2)

            @pl.when(n + 1 < 8)
            def _():
                arrived(n + 1)
                fetch(n + 1, 1 - slot)

            pltpu.make_async_copy(
                u4.at[pl.ds(0, UNIT), :], stage.at[slot], stage_sem.at[slot]
            ).wait()
            unit, half = unit_of(n)
            for i in range(2):
                block = half * 8 + unit * 2 + i
                quarter, j = block // 4, lax.rem(block, 4)
                to = (2 * quarter + lax.rem(j, 2)) * 2 + j // 2
                hi, lo = halves(stage[slot, i * BS : i * BS + BS, :])
                uhi[block_at(to, BS), :] = hi
                ulo[block_at(to, BS), :] = lo
            return carry

        arrived(0)
        fetch(0, 0)
        lax.fori_loop(0, 8, step, 0)

    def level(depth):
        last = depth == 3
        at = depth % 2
        hq, pq, ptl = ((hq0, pq0, ptl0), (hq1, pq1, ptl1))[at]
        for r in range(2):
            for b in range(16):
                value = held[r, b]
                hi, lo = halves(value)
                hs[r * BS : r * BS + BS, b * BS : b * BS + BS] = hi
                hs[256 + r * BS : 256 + r * BS + BS, b * BS : b * BS + BS] = lo
                hq[2 * r + c, b] = value
            pair_copy(hq, at, r, hx_s, hx_r).start()
        if not last:
            gathers[depth].collect()
        split_update(depth)

        def piece(to):
            return remote(
                st.at[to], ptl.at[pl.ds(2 * e, 2)], ps.at[to], pr.at[at, e],
                device(z, y, to // 2, lax.rem(to, 2)),
            )

        def panel_step(k, carry):
            step = jnp.where(k == 0, 2, jnp.where(k == 1, 1, jnp.where(k == 2, 3, 0)))
            t = lax.rem(q + step, 4)
            cols = block_at(t, 256)
            both = dot(hs[...], uhi[:, cols])
            part = both[:256] + both[256:] + dot(hs[:256, :], ulo[:, cols])
            for r in range(2):
                pq[2 * r + c, :, cols] = part[r * BS : r * BS + BS]
            for core in range(2):
                to = 2 * t + core
                turned = [
                    part[r * BS : r * BS + BS, core * BS : core * BS + BS].T for r in range(2)
                ]

                @pl.when(to == e)
                def _():
                    for r in range(2):
                        ptl[2 * e + r] = turned[r]

                @pl.when(to != e)
                def _():
                    for r in range(2):
                        st[to, r] = turned[r]
                    piece(to).start()

            return carry

        lax.fori_loop(0, 4, panel_step, 0)
        for r in range(2):
            pair_copy(pq, at, r, px_s, px_r).start()
        if last:
            v4_copy().wait()
            acc[0] = acc[1]
        else:
            acc[0] = vg[depth]

        def square_step(s, carry):
            k = s // 2
            step = jnp.where(k == 0, 0, jnp.where(k == 1, 1, jnp.where(k == 2, 3, 2)))
            m = 2 * lax.rem(q + step, 4) + lax.rem(s + c, 2)

            @pl.when(m != e)
            def _():
                there = ptl.at[pl.ds(2 * m, 2)]
                remote(there, there, ps.at[m], pr.at[at, m], partner).wait_recv()

            hi, lo = halves(jnp.concatenate([ptl[2 * m], ptl[2 * m + 1]], 1))
            rows = block_at(m, 256)
            both = dot(jnp.concatenate([hi, lo], 0), uhi[rows, :])
            acc[0] += both[:BS] + both[BS:] + dot(hi, ulo[rows, :])
            return carry

        lax.fori_loop(0, 8, square_step, 0)
        for r in range(2):
            pair_arrived(hq, at, r, hx_s, hx_r).wait_recv()
            pair_arrived(pq, at, r, px_s, px_r).wait_recv()

        if not last:
            chosen = sel_ref[16 * depth + e]
            for m in range(8):
                block = sel_ref[16 * depth + 8 + m]
                held[0, 2 * m] = acc[0, :, m * BS : m * BS + BS]
                held[0, 2 * m + 1] = -ptl[block]
                held[1, 2 * m] = -pq[chosen, :, m * BS : m * BS + BS]
                held[1, 2 * m + 1] = hq[chosen, block]
        else:

            def rows_of(half):
                for p in range(2):
                    quarter = 2 * half + p
                    yield p * 768, acc[0, :, block_at(quarter, 256)]
                    for a in range(4):
                        yield p * 768 + 256 + a * BS, -ptl[2 * (2 * quarter + a % 2) + a // 2]

            for to, value in rows_of(1 - c):
                xin[1, :, to : to + value.shape[1]] = value
            cross = remote(xin.at[1], xin.at[0], xs_s, xs_r, partner)
            cross.start()
            for to, value in rows_of(c):
                out_ref[0, block_at(c, BS), to : to + value.shape[1]] = value
            for a in range(4):
                rows = slice(256 + a * BS, 256 + a * BS + BS)
                for p in range(2):
                    quarter = 2 * c + p
                    out_ref[0, rows, p * 768 : p * 768 + 256] = -pq[a, :, block_at(quarter, 256)]
                    for b in range(4):
                        block = 2 * (2 * quarter + b % 2) + b // 2
                        to = p * 768 + 256 + b * BS
                        out_ref[0, rows, to : to + BS] = hq[a, block]
            cross.wait()
            out_ref[0, block_at(1 - c, BS), :] = xin[0]

        for r in range(2):
            pair_copy(hq, at, r, hx_s, hx_r).wait_send()
            pair_copy(pq, at, r, px_s, px_r).wait_send()

        def sent(to, carry):
            @pl.when(to != e)
            def _():
                piece(to).wait_send()

            return carry

        lax.fori_loop(0, 8, sent, 0)

    level(0)
    g2.share_out()
    g3.send()
    level(1)
    g3.share_out()
    level(2)
    level(3)
    for g in gathers:
        g.finish()
    for unit in range(4):
        u4_push(unit).wait_send()


def whole(tab, mask, sel, root, updates, pivots):
    dma = pltpu.SemaphoreType.DMA
    any_space = pl.BlockSpec(memory_space=pl.ANY)
    smem = pl.BlockSpec(memory_space=pltpu.SMEM)
    gather_sems = []
    for depth in range(3):
        n = 8 >> depth
        gather_sems += [
            dma((2,)), dma((n,)), dma((n,)), dma((3, n)), dma((3, n)), dma((4,)), dma((4,)), dma((n,)), dma((n,)),
        ]
    outs = pl.pallas_call(
        whole_kernel,
        out_shape=[jax.ShapeDtypeStruct((1, 768, 1536), F32)]
        + [jax.ShapeDtypeStruct((2, 1024, 1024), F32)] * 3
        + [jax.ShapeDtypeStruct((1024, 1024), F32)],
        in_specs=[smem] * 3 + [any_space] * 9,
        out_specs=[pl.BlockSpec(memory_space=pltpu.VMEM)] + [any_space] * 4,
        scratch_shapes=[
            pltpu.VMEM((16, 8, BS, BS), F32),
            pltpu.VMEM((2, 4, 4, BS, BS), F32),
            pltpu.VMEM((4, 4, BS, BS), F32),
            pltpu.VMEM((4, 4, BS, BS), F32),
            pltpu.VMEM((3, 4, BS, BS), F32),
            pltpu.VMEM((4, BS, BS), F32),
            pltpu.VMEM((2, 16, BS, BS), F32),
            pltpu.VMEM((4, 16, BS, BS), F32),
            pltpu.VMEM((4, 16, BS, BS), F32),
            pltpu.VMEM((4, BS, SEP), F32),
            pltpu.VMEM((4, BS, SEP), F32),
            pltpu.VMEM((16, BS, BS), F32),
            pltpu.VMEM((16, BS, BS), F32),
            pltpu.VMEM((ANC, SEP), BF16),
            pltpu.VMEM((ANC, SEP), BF16),
            pltpu.VMEM((2, UNIT, SEP), F32),
            pltpu.VMEM((512, ANC), BF16),
            pltpu.VMEM((8, 2, BS, BS), F32),
            pltpu.VMEM((3, BS, SEP), F32),
            pltpu.VMEM((2, BS, SEP), F32),
            pltpu.VMEM((2, BS, 1536), F32),
            dma((16,)),
            dma,
            dma,
            dma((3,)),
            dma((3,)),
            dma((8,)),
            dma((8,)),
        ]
        + gather_sems
        + [
            dma((4,)),
            dma((4,)),
            dma,
            dma((2,)),
            dma((8,)),
            dma((2, 8)),
            dma((2, 2)),
            dma((2, 2)),
            dma((2, 2)),
            dma((2, 2)),
            dma,
            dma,
        ],
        compiler_params=pltpu.CompilerParams(
            collective_id=0, has_side_effects=True, vmem_limit_bytes=60 * 2**20
        ),
        name="whole",
    )(tab, mask, sel, root, *updates, *pivots)
    return outs[0]


def shards(
    root_inverse,
    blocks_one,
    blocks_two,
    blocks_three,
    blocks_four,
    update_one,
    update_two,
    update_three,
    update_four,
    pivot_one,
    pivot_two,
    pivot_three,
    pivot_four,
):
    z, y, x, c = place()
    leaf = z * 4 + y
    rows = lax.dynamic_slice_in_dim(blocks_one, z * 4, 4, 1)[:, None, :] - leaf * 8
    cols = lax.dynamic_slice_in_dim(blocks_one, x * 4, 4, 1)[:, :, None] - (x * 2 + c) * 16
    rows, cols = jnp.broadcast_arrays(rows, cols)
    valid = (rows >= 0) & (rows < 8) & (cols >= 0) & (cols < 16)
    tab = jnp.concatenate([jnp.clip(rows, 0, 7).reshape(32), jnp.clip(cols, 0, 15).reshape(32)])
    mask = valid.reshape(32).astype(F32)
    quarters = jnp.arange(8, dtype=jnp.int32) // 2
    sel = []
    for depth, lists in enumerate((blocks_two, blocks_three, blocks_four)):
        ids = lax.dynamic_index_in_dim(lists, leaf // (4 >> depth), 0, keepdims=False)
        chosen = jnp.clip(ids.reshape(4, 4)[:, 2:].reshape(8) - 6 * quarters - 2, 0, 3)
        sel += [chosen, 4 * quarters + 2 * (chosen % 2) + chosen // 2]
    return whole(
        tab,
        mask,
        jnp.concatenate(sel),
        root_inverse.reshape(8, BS, 2048),
        (update_one, update_two, update_three, update_four),
        (pivot_one, pivot_two, pivot_three, pivot_four),
    )


def solution(mesh):
    mesh = Mesh(mesh.devices.reshape(2, 2, 2, 2, 4, 2), AXES)
    leaf = AXES[:4]
    placed = (
        P(leaf, ("row", "col")),
        P(),
        P(),
        P(),
        P(),
        P("col", leaf),
        P("col", leaf),
        P("col", leaf),
        P("col", leaf),
        P("row", leaf),
        P("row", leaf),
        P("row", leaf),
        P("row", leaf),
    )
    return jax.shard_map(
        shards, mesh=mesh, in_specs=placed, out_specs=P(leaf, "row", "col"), check_vma=False
    )
```

```python
import jax
import jax.numpy as jnp
from jax import lax
from jax.experimental import pallas as pl
from jax.experimental.pallas import tpu as pltpu
from jax.sharding import Mesh, PartitionSpec as P

SEP = 1024
ANC = 2048
BS = 128
UNIT = 256
AXES = ("za", "zb", "ya", "yb", "row", "col")
MESH = pl.DeviceIdType.MESH
F32 = jnp.float32
BF16 = jnp.bfloat16


def place():
    z = lax.axis_index("za") * 2 + lax.axis_index("zb")
    y = lax.axis_index("ya") * 2 + lax.axis_index("yb")
    return z, y, lax.axis_index("row"), lax.axis_index("col")


def device(z, y, x, c):
    return (z // 2, z % 2, y // 2, y % 2, x, c)


def halves(value):
    high = value.astype(BF16)
    return high, (value - high.astype(F32)).astype(BF16)


def dot(a, b):
    return jnp.dot(a, b, preferred_element_type=F32)


def block_at(index, size):
    return pl.ds(pl.multiple_of(index * size, size), size)


def remote(src, dst, send, recv, to):
    return pltpu.make_async_remote_copy(
        src_ref=src, dst_ref=dst, send_sem=send, recv_sem=recv, device_id=to, device_id_type=MESH
    )


class Gather:
    def __init__(self, level, spot, u, v, ug, vg, sems):
        self.level, self.u, self.v, self.ug, self.vg = level, u, v, ug, vg
        self.z, self.y, self.x, self.c = spot
        self.own_sem, self.a_s, self.a_r, self.b_s, self.b_r, self.c_s, self.c_r, self.v_s, self.v_r = sems
        self.count = 8 >> level
        self.width = SEP // self.count
        self.me = lax.rem(self.z * 4 + self.y, self.count)
        self.first = self.x
        self.units = 1

    def peer(self, d):
        base = (self.z * 4 + self.y) // self.count * self.count
        return lax.rem(self.me + d, self.count), base

    def leaf(self, member, base):
        at = base + member
        return device(at // 4, lax.rem(at, 4), self.x, self.c)

    def cols(self, member):
        return block_at(member, self.width)

    def rows(self, first, units):
        return pl.ds(pl.multiple_of(first * UNIT, UNIT), units * UNIT)

    def own(self):
        return (
            pltpu.make_async_copy(self.u, self.ug.at[self.c, :, self.cols(self.me)], self.own_sem.at[0]),
            pltpu.make_async_copy(
                self.v.at[block_at(self.c, BS), :], self.vg.at[:, self.cols(self.me)], self.own_sem.at[1]
            ),
        )

    def a_copy(self, d):
        member, base = self.peer(d)
        rows = self.rows(self.first, self.units)
        return remote(
            self.u.at[rows, :], self.ug.at[self.c, rows, self.cols(self.me)],
            self.a_s.at[d], self.a_r.at[self.me], self.leaf(member, base),
        )

    def v_copy(self, d):
        member, base = self.peer(d)
        return remote(
            self.v.at[block_at(self.c, BS), :], self.vg.at[:, self.cols(self.me)],
            self.v_s.at[d], self.v_r.at[self.me], self.leaf(member, base),
        )

    def a_arrived(self, member):
        rows = self.rows(self.first, self.units)
        there = self.ug.at[self.c, rows, self.cols(member)]
        return remote(there, there, self.a_s.at[0], self.a_r.at[member], device(self.z, self.y, self.x, 1 - self.c))

    def v_arrived(self, member):
        there = self.vg.at[:, self.cols(member)]
        return remote(there, there, self.v_s.at[0], self.v_r.at[member], device(self.z, self.y, self.x, 1 - self.c))

    def b_place(self, n, member, source):
        if n < 2:
            rows = self.rows(source, 1)
        else:
            unit = lax.rem(source + (3, 1)[n - 2], 4)
            rows = pl.ds(pl.multiple_of(unit * UNIT + (n - 2) * BS, BS), BS)
        return self.ug.at[self.c, rows, self.cols(member)]

    def b_copy(self, n, member):
        there = self.b_place(n, member, self.x)
        to = device(self.z, self.y, lax.rem(self.x + (1, 3)[n % 2], 4), self.c)
        return remote(there, there, self.b_s.at[n, member], self.b_r.at[n, member], to)

    def b_arrived(self, n, member):
        there = self.b_place(n, member, lax.rem(self.x + (3, 1)[n % 2], 4))
        return remote(
            there, there, self.b_s.at[n, member], self.b_r.at[n, member],
            device(self.z, self.y, self.x, 1 - self.c),
        )

    def c_copy(self, unit, half):
        there = self.ug.at[half, self.rows(unit, 1), :]
        return remote(
            there, there, self.c_s.at[unit], self.c_r.at[unit], device(self.z, self.y, self.x, 1 - self.c)
        )

    def begin(self):
        for copy in self.own():
            copy.start()

    def send(self):
        for d in range(1, self.count):
            self.a_copy(d).start()

    def send_pivot(self):
        for d in range(1, self.count):
            self.v_copy(d).start()

    def others(self, body):
        def step(d, carry):
            body(lax.rem(self.me + self.count - d, self.count))
            return carry

        lax.fori_loop(1, self.count, step, 0)

    def share_out(self):
        for copy in self.own():
            copy.wait()

        def body(member):
            self.a_arrived(member).wait_recv()
            for n in range(2):
                self.b_copy(n, member).start()

        self.others(body)
        self.c_copy(self.x, self.c).start()

    def forward(self):
        def body(member):
            for n in range(2):
                self.b_arrived(n, member).wait_recv()
                self.b_copy(2 + n, member).start()

        self.others(body)
        for step in (3, 1):
            self.c_copy(lax.rem(self.x + step, 4), self.c).start()

    def collect(self):
        def body(member):
            for n in range(2, 4):
                self.b_arrived(n, member).wait_recv()

        self.others(body)
        self.c_copy(lax.rem(self.x + 2, 4), self.c).start()

    def collect_pivot(self):
        def step(d, carry):
            self.v_arrived(lax.rem(self.me + self.count - d, self.count)).wait_recv()
            return carry

        lax.fori_loop(1, self.count, step, 0)

    def wait_other(self, unit):
        self.c_copy(unit, 1 - self.c).wait_recv()

    def finish(self):
        def step(d, carry):
            self.a_copy(d).wait_send()
            self.v_copy(d).wait_send()
            return carry

        lax.fori_loop(1, self.count, step, 0)

        def body(member):
            for n in range(4):
                self.b_copy(n, member).wait_send()

        self.others(body)
        for unit in range(4):
            self.c_copy(unit, self.c).wait_send()


def whole_kernel(
    one_ref, two_ref, three_ref, four_ref, root_ref, u1, u2, u3, u4, v1, v2, v3, v4,
    out_ref, ug1, ug3, ug4,
    core_in, mine, y_in, ready, held, hq0, hq1, pq0, pq1, ptl0, ptl1,
    u2v, u2hi, u2lo, uhi0, ulo0, stage, hs, st, vg, acc, sq, xin,
    root_sem, core_s, core_r, ys, yr, h_s, h_r,
    own1, a1s, a1r, b1s, b1r, c1s, c1r, w1s, w1r,
    own3, a3s, a3r, b3s, b3r, c3s, c3r, w3s, w3r,
    c4s, c4r, v4_sem, u2_own, u2_s, u2_r, ag_s, ag_r, sg_s, sg_r,
    stage_sem, ps, pr, psr, prr, hx_s, hx_r, px_s, px_r, xs_s, xs_r,
):
    spot = place()
    z, y, q, c = spot
    e = 2 * q + c
    partner = device(z, y, q, 1 - c)
    g1 = Gather(0, spot, u1, v1, ug1, vg.at[0], (own1, a1s, a1r, b1s, b1r, c1s, c1r, w1s, w1r))
    g3 = Gather(2, spot, u3, v3, ug3, vg.at[1], (own3, a3s, a3r, b3s, b3r, c3s, c3r, w3s, w3r))
    gathers = (g1, None, g3)
    leaf = z * 4 + y

    def peer(dy):
        return device(z, lax.rem(y + dy, 4), q, c)

    def picked_from(f, j, i):
        row = one_ref[f, 4 * z + i] - leaf * 8
        col = one_ref[f, 4 * q + j] - e * 16
        here = (row >= 0) & (row < 8) & (col >= 0) & (col < 16)
        return (
            jnp.minimum(jnp.maximum(col, 0), 15),
            jnp.minimum(jnp.maximum(row, 0), 7),
            jnp.where(here, 1.0, 0.0),
        )

    def chosen_block(depth, m):
        ids = (two_ref, three_ref, four_ref)[depth]
        quarter = m // 2
        block = ids[leaf // (4 >> depth), 4 * quarter + 2 + m % 2] - 6 * quarter - 2
        return jnp.minimum(jnp.maximum(block, 0), 3)

    def member_block(m, a):
        return 4 * (m // 2) + 2 * lax.rem(a, 2) + a // 2

    barrier = pltpu.get_barrier_semaphore()

    def signal(dev):
        pl.semaphore_signal(barrier, inc=1, device_id=dev, device_id_type=MESH)

    mine_f = z // 2

    def u2_own_copy():
        return pltpu.make_async_copy(u2, u2v.at[c], u2_own.at[0])

    def v2_own_copy():
        return pltpu.make_async_copy(v2.at[block_at(c, BS), :], sq.at[:, block_at(y, 256)], u2_own.at[1])

    def u2_push():
        return remote(u2, u2v.at[c], u2_s, u2_r, partner)

    def u4_push(unit):
        rows = pl.ds(unit * UNIT, UNIT)
        return remote(u4.at[rows, :], ug4.at[rows, :], c4s.at[unit], c4r.at[unit], partner)

    def v4_copy():
        return pltpu.make_async_copy(v4.at[block_at(c, BS), :], acc.at[1], v4_sem)

    def enter():
        g1.begin()
        g3.begin()
        u2_own_copy().start()
        v2_own_copy().start()
        for t in range(8):

            @pl.when(t != e)
            def _():
                signal(device(z, y, t // 2, t % 2))

        for d in range(1, 8):
            member, base = g1.peer(d)
            signal(g1.leaf(member, base))
        for p in range(4):
            for r in range(2):
                j = 2 * r + c

                @pl.when(jnp.logical_not((p == z) & (j == y) & (mine_f == c)))
                def _():
                    signal(device(p, j, q, mine_f))

        own = (mine_f == c) & (y % 2 == c)
        pl.semaphore_wait(barrier, jnp.where(own, 21, 22))

        g1.send()

        u2_push().start()

        for unit in range(4):
            u4_push(unit).start()
        v4_copy().start()

    def split_update(depth, uhi, ulo, start, stop):
        def unit_of(n):
            k = n // 2
            step = jnp.where(k == 0, 0, jnp.where(k == 1, 3, jnp.where(k == 2, 1, 2)))
            return lax.rem(q + step, 4), lax.rem(n + c, 2)

        def fetch(n, slot):
            unit, half = unit_of(n)
            rows = pl.ds(pl.multiple_of(unit * UNIT, UNIT), UNIT)
            if depth < 3:
                pltpu.make_async_copy(
                    gathers[depth].ug.at[half, rows, :], stage.at[slot], stage_sem.at[slot]
                ).start()
            else:

                @pl.when(half == c)
                def _():
                    pltpu.make_async_copy(u4.at[rows, :], stage.at[slot], stage_sem.at[slot]).start()

                @pl.when(half != c)
                def _():
                    pltpu.make_async_copy(ug4.at[rows, :], stage.at[slot], stage_sem.at[slot]).start()

        def arrived(n):
            unit, half = unit_of(n)

            @pl.when(half != c)
            def _():
                if depth < 3:
                    gathers[depth].wait_other(unit)
                else:
                    rows = pl.ds(pl.multiple_of(unit * UNIT, UNIT), UNIT)
                    remote(
                        ug4.at[rows, :], ug4.at[rows, :], c4s.at[unit], c4r.at[unit], partner
                    ).wait_recv()

        def step(n, carry):
            slot = lax.rem(n, 2)

            @pl.when(n + 1 < stop)
            def _():
                arrived(n + 1)
                fetch(n + 1, 1 - slot)

            pltpu.make_async_copy(
                u4.at[pl.ds(0, UNIT), :], stage.at[slot], stage_sem.at[slot]
            ).wait()
            unit, half = unit_of(n)
            for i in range(2):
                block = half * 8 + unit * 2 + i
                quarter, j = block // 4, lax.rem(block, 4)
                to = (2 * quarter + lax.rem(j, 2)) * 2 + j // 2
                hi, lo = halves(stage[slot, i * BS : i * BS + BS, :])
                uhi[block_at(to, BS), :] = hi
                ulo[block_at(to, BS), :] = lo
            return carry

        arrived(start)
        fetch(start, start % 2)
        lax.fori_loop(start, stop, step, 0)

    def take(rootv, picked):
        def root_copy(j):
            return pltpu.make_async_copy(
                root_ref.at[:, :, j * BS : j * BS + BS], rootv.at[j], root_sem.at[j]
            )

        for j in range(16):
            root_copy(j).start()
        enter()
        for j in range(16):
            root_copy(j).wait()

        def pick(n, carry):
            f, j = n // 4, n % 4
            for i in range(4):
                col, row, here = picked_from(f, j, i)
                picked[f, j, i % 2 * 2 + i // 2] = (rootv[col, row] * here).T
            return carry

        lax.fori_loop(0, 8, pick, 0)
        core = remote(picked.at[1 - c], core_in, core_s, core_r, partner)
        core.start()
        core.wait()
        mine[...] = picked[c] + core_in[...]

    pl.run_scoped(
        take, pltpu.VMEM((16, 8, BS, BS), F32), pltpu.VMEM((2, 4, 4, BS, BS), F32)
    )

    def y_copy(d):
        to = lax.rem(y + d, 4)
        return remote(mine.at[to], y_in.at[d - 1], ys.at[d - 1], yr.at[d - 1], device(z, to, q, c))

    for d in (2, 1, 3):
        y_copy(d).start()
    g1.share_out()
    for d in (1, 3, 2):
        y_copy(d).wait()
    ready[...] = mine[y] + y_in[0] + y_in[1] + y_in[2]

    def h_copy(k, d):
        return remote(
            ready, held.at[y // 2, pl.ds(4 * z, 4)], h_s.at[k * 4 + d], h_r.at[z * 2 + y // 2],
            device(2 * c + k, lax.rem(y + d, 4), q, y % 2),
        )

    def to_self(k):
        return (2 * c + k == z) & (y % 2 == c)

    for d in (2, 1, 3):
        for k in range(2):
            h_copy(k, d).start()
    for k in range(2):

        @pl.when(jnp.logical_not(to_self(k)))
        def _():
            h_copy(k, 0).start()

        @pl.when(to_self(k))
        def _():
            held[y // 2, pl.ds(4 * z, 4)] = ready[...]

    u2_own_copy().wait()
    u2_push().wait()

    def split_two(b, carry):
        m = b // 2
        src = 4 * (m // 2) + 2 * lax.rem(b, 2) + lax.rem(m, 2)
        hi, lo = halves(u2v[src // 8, block_at(lax.rem(src, 8), BS), :])
        u2hi[block_at(b, BS), :] = hi
        u2lo[block_at(b, BS), :] = lo
        return carry

    lax.fori_loop(0, 16, split_two, 0)
    g1.forward()
    split_update(0, uhi0, ulo0, 0, 6)
    for p in range(4):
        for r in range(2):

            @pl.when(jnp.logical_not((p == z) & (2 * r + c == y) & (mine_f == c)))
            def _():
                there = held.at[r, pl.ds(4 * p, 4)]
                remote(there, there, h_s.at[0], h_r.at[p * 2 + r], partner).wait_recv()

    for d in (2, 1, 3):
        for k in range(2):
            h_copy(k, d).wait_send()
    for k in range(2):

        @pl.when(jnp.logical_not(to_self(k)))
        def _():
            h_copy(k, 0).wait_send()

    def pair_copy(ref, at, r, s_sem, r_sem):
        return remote(
            ref.at[2 * r + c], ref.at[2 * r + c], s_sem.at[at, r], r_sem.at[at, r], partner
        )

    def pair_arrived(ref, at, r, s_sem, r_sem):
        there = ref.at[2 * r + 1 - c]
        return remote(there, there, s_sem.at[at, r], r_sem.at[at, r], partner)

    def begin_level(at):
        hq = (hq0, hq1)[at]
        for r in range(2):
            for b in range(16):
                value = held[r, b]
                hi, lo = halves(value)
                hs[r * BS : r * BS + BS, b * BS : b * BS + BS] = hi
                hs[256 + r * BS : 256 + r * BS + BS, b * BS : b * BS + BS] = lo
                hq[2 * r + c, b] = value
            pair_copy(hq, at, r, hx_s, hx_r).start()

    def piece_copy(at, to):
        return remote(
            st.at[to], (ptl0, ptl1)[at].at[pl.ds(2 * e, 2)], ps.at[to], pr.at[at, e],
            device(z, y, to // 2, lax.rem(to, 2)),
        )

    def give(at, to, turned):
        ptl = (ptl0, ptl1)[at]

        @pl.when(to == e)
        def _():
            for r in range(2):
                ptl[2 * e + r] = turned[r]

        @pl.when(to != e)
        def _():
            for r in range(2):
                st[to, r] = turned[r]
            piece_copy(at, to).start()

    def part_copy(at, to, r):
        return remote(
            st.at[to, r], (ptl0, ptl1)[at].at[2 * e + r], psr.at[to, r], prr.at[e, r],
            device(z, y, to // 2, lax.rem(to, 2)),
        )

    def give_part(at, to, r, turned):
        ptl = (ptl0, ptl1)[at]

        @pl.when(to == e)
        def _():
            ptl[2 * e + r] = turned

        @pl.when(to != e)
        def _():
            st[to, r] = turned
            part_copy(at, to, r).start()

    def square_loop(at, out, cols, uhi, ulo, parts):
        ptl = (ptl0, ptl1)[at]

        def square_step(s, carry):
            k = s // 2
            step = jnp.where(k == 0, 0, jnp.where(k == 1, 1, jnp.where(k == 2, 3, 2)))
            m = 2 * lax.rem(q + step, 4) + lax.rem(s + c, 2)

            @pl.when(m != e)
            def _():
                if parts:
                    for r in range(2):
                        there = ptl.at[2 * m + r]
                        remote(there, there, psr.at[m, r], prr.at[m, r], partner).wait_recv()
                else:
                    there = ptl.at[pl.ds(2 * m, 2)]
                    remote(there, there, ps.at[m], pr.at[at, m], partner).wait_recv()

            hi, lo = halves(jnp.concatenate([ptl[2 * m], ptl[2 * m + 1]], 1))
            rows = block_at(m, 256)
            both = dot(jnp.concatenate([hi, lo], 0), uhi[rows, :])
            out[:, cols] += both[:BS] + both[BS:] + dot(hi, ulo[rows, :])
            return carry

        lax.fori_loop(0, 8, square_step, 0)

    def next_held(depth, at, square):
        hq, pq, ptl = ((hq0, pq0, ptl0), (hq1, pq1, ptl1))[at]
        for r in range(2):
            pair_arrived(hq, at, r, hx_s, hx_r).wait_recv()
            pair_arrived(pq, at, r, px_s, px_r).wait_recv()
        chosen = chosen_block(depth, e)
        for m in range(8):
            block = member_block(m, chosen_block(depth, m))
            held[0, 2 * m] = square[:, m * BS : m * BS + BS]
            held[0, 2 * m + 1] = -ptl[block]
            held[1, 2 * m] = -pq[chosen, :, m * BS : m * BS + BS]
            held[1, 2 * m + 1] = hq[chosen, block]

    def end_level(at, parts):
        hq, pq = ((hq0, pq0), (hq1, pq1))[at]
        for r in range(2):
            pair_copy(hq, at, r, hx_s, hx_r).wait_send()
            pair_copy(pq, at, r, px_s, px_r).wait_send()

        def sent(to, carry):
            @pl.when(to != e)
            def _():
                if parts:
                    for r in range(2):
                        part_copy(at, to, r).wait_send()
                else:
                    piece_copy(at, to).wait_send()

            return carry

        lax.fori_loop(0, 8, sent, 0)

    def level_two(later):
        pq = pq1
        begin_level(1)
        cols = block_at(y, 256)
        both = dot(hs[...], u2hi[...])
        part = both[:256] + both[256:] + dot(hs[:256, :], u2lo[...])

        def panel_out(dy, r):
            rows = pq.at[2 * r + c, :, cols]
            return remote(rows, rows, ag_s.at[dy, r], ag_r.at[y, r], peer(dy))

        def turn(m, r):
            for core in range(2):
                value = pq[2 * r + c, :, pl.ds(pl.multiple_of(m * 256 + core * BS, BS), BS)]
                give_part(1, 2 * m + core, r, value.T)

        for r in range(2):
            pq[2 * r + c, :, cols] = part[r * BS : r * BS + BS]
        for dy in (1, 3, 2):
            panel_out(dy, 0).start()
        turn(y, 0)
        turn(y, 1)
        for dy in (1, 3, 2):
            panel_out(dy, 0).wait_send()
        for dy in (1, 3, 2):
            panel_out(dy, 1).start()
        for r in range(2):
            for dy in (1, 3, 2):
                m = lax.rem(y + dy, 4)
                there = pq.at[2 * r + c, :, block_at(m, 256)]
                remote(there, there, ag_s.at[0, r], ag_r.at[m, r], partner).wait_recv()
                turn(m, r)
        for r in range(2):
            pair_copy(pq, 1, r, px_s, px_r).start()
        g3.forward()
        v2_own_copy().wait()
        square_loop(1, sq, cols, u2hi, u2lo, True)

        def square_out(dy):
            return remote(sq.at[:, cols], sq.at[:, cols], sg_s.at[dy], sg_r.at[y], peer(dy))

        for dy in (1, 3, 2):
            square_out(dy).start()
        later()
        for dy in (1, 3, 2):
            panel_out(dy, 1).wait_send()
            m = lax.rem(y + dy, 4)
            there = sq.at[:, block_at(m, 256)]
            remote(there, there, sg_s.at[0], sg_r.at[m], partner).wait_recv()
        next_held(1, 1, sq)
        for dy in (1, 3, 2):
            square_out(dy).wait_send()
        end_level(1, True)

    def level(depth, uhi, ulo, early, meanwhile):
        last = depth == 3
        at = depth % 2
        hq, pq, ptl = ((hq0, pq0, ptl0), (hq1, pq1, ptl1))[at]
        begin_level(at)
        early()

        def panel_step(k, carry):
            step = jnp.where(k == 0, 2, jnp.where(k == 1, 1, jnp.where(k == 2, 3, 0)))
            t = lax.rem(q + step, 4)
            cols = block_at(t, 256)
            both = dot(hs[...], uhi[:, cols])
            part = both[:256] + both[256:] + dot(hs[:256, :], ulo[:, cols])
            for r in range(2):
                pq[2 * r + c, :, cols] = part[r * BS : r * BS + BS]
            for core in range(2):
                turned = [
                    part[r * BS : r * BS + BS, core * BS : core * BS + BS].T for r in range(2)
                ]
                give(at, 2 * t + core, turned)
            return carry

        lax.fori_loop(0, 4, panel_step, 0)
        for r in range(2):
            pair_copy(pq, at, r, px_s, px_r).start()
        meanwhile()
        if last:
            v4_copy().wait()
            acc[0] = acc[1]
        else:
            gathers[depth].collect_pivot()
            acc[0] = vg[depth // 2]
        square_loop(at, acc.at[0], slice(None), uhi, ulo, False)
        if not last:
            next_held(depth, at, acc.at[0])
        else:
            for r in range(2):
                pair_arrived(hq, at, r, hx_s, hx_r).wait_recv()
                pair_arrived(pq, at, r, px_s, px_r).wait_recv()

            def rows_of(half):
                for p in range(2):
                    quarter = 2 * half + p
                    yield p * 768, acc[0, :, block_at(quarter, 256)]
                    for a in range(4):
                        yield p * 768 + 256 + a * BS, -ptl[2 * (2 * quarter + a % 2) + a // 2]

            for to, value in rows_of(1 - c):
                xin[1, :, to : to + value.shape[1]] = value
            cross = remote(xin.at[1], xin.at[0], xs_s, xs_r, partner)
            cross.start()
            for to, value in rows_of(c):
                out_ref[0, block_at(c, BS), to : to + value.shape[1]] = value
            for a in range(4):
                rows = slice(256 + a * BS, 256 + a * BS + BS)
                for p in range(2):
                    quarter = 2 * c + p
                    out_ref[0, rows, p * 768 : p * 768 + 256] = -pq[a, :, block_at(quarter, 256)]
                    for b in range(4):
                        block = 2 * (2 * quarter + b % 2) + b // 2
                        to = p * 768 + 256 + b * BS
                        out_ref[0, rows, to : to + BS] = hq[a, block]
            cross.wait()
            out_ref[0, block_at(1 - c, BS), :] = xin[0]

        end_level(at, False)

    def levels(uhi1, ulo1):
        def rest_of_one():
            g1.collect()
            split_update(0, uhi0, ulo0, 6, 8)

        def three():
            g3.collect()
            split_update(2, uhi1, ulo1, 0, 8)

        g1.send_pivot()
        g3.send()
        g3.send_pivot()
        level(0, uhi0, ulo0, rest_of_one, lambda: None)
        g3.share_out()
        level_two(three)
        level(2, uhi1, ulo1, lambda: None, lambda: split_update(3, uhi0, ulo0, 0, 8))
        level(3, uhi0, ulo0, lambda: None, lambda: None)

    pl.run_scoped(levels, pltpu.VMEM((ANC, SEP), BF16), pltpu.VMEM((ANC, SEP), BF16))
    g1.finish()
    g3.finish()
    for unit in range(4):
        u4_push(unit).wait_send()


def whole(blocks, root, updates, pivots):
    dma = pltpu.SemaphoreType.DMA
    any_space = pl.BlockSpec(memory_space=pl.ANY)
    smem = pl.BlockSpec(memory_space=pltpu.SMEM)
    gather_sems = []
    for n in (8, 2):
        gather_sems += [
            dma((2,)), dma((n,)), dma((n,)), dma((4, n)), dma((4, n)), dma((4,)), dma((4,)), dma((n,)), dma((n,)),
        ]
    outs = pl.pallas_call(
        whole_kernel,
        out_shape=[jax.ShapeDtypeStruct((1, 768, 1536), F32)]
        + [jax.ShapeDtypeStruct((2, 1024, 1024), F32)] * 2
        + [jax.ShapeDtypeStruct((1024, 1024), F32)],
        in_specs=[smem] * 4 + [any_space] * 9,
        out_specs=[pl.BlockSpec(memory_space=pltpu.VMEM)] + [any_space] * 3,
        scratch_shapes=[
            pltpu.VMEM((4, 4, BS, BS), F32),
            pltpu.VMEM((4, 4, BS, BS), F32),
            pltpu.VMEM((3, 4, BS, BS), F32),
            pltpu.VMEM((4, BS, BS), F32),
            pltpu.VMEM((2, 16, BS, BS), F32),
            pltpu.VMEM((4, 16, BS, BS), F32),
            pltpu.VMEM((4, 16, BS, BS), F32),
            pltpu.VMEM((4, BS, SEP), F32),
            pltpu.VMEM((4, BS, SEP), F32),
            pltpu.VMEM((16, BS, BS), F32),
            pltpu.VMEM((16, BS, BS), F32),
            pltpu.VMEM((2, 1024, 256), F32),
            pltpu.VMEM((ANC, 256), BF16),
            pltpu.VMEM((ANC, 256), BF16),
            pltpu.VMEM((ANC, SEP), BF16),
            pltpu.VMEM((ANC, SEP), BF16),
            pltpu.VMEM((2, UNIT, SEP), F32),
            pltpu.VMEM((512, ANC), BF16),
            pltpu.VMEM((8, 2, BS, BS), F32),
            pltpu.VMEM((2, BS, SEP), F32),
            pltpu.VMEM((2, BS, SEP), F32),
            pltpu.VMEM((BS, SEP), F32),
            pltpu.VMEM((2, BS, 1536), F32),
            dma((16,)),
            dma,
            dma,
            dma((3,)),
            dma((3,)),
            dma((8,)),
            dma((8,)),
        ]
        + gather_sems
        + [
            dma((4,)),
            dma((4,)),
            dma,
            dma((2,)),
            dma,
            dma,
            dma((4, 2)),
            dma((4, 2)),
            dma((4,)),
            dma((4,)),
            dma((2,)),
            dma((8,)),
            dma((2, 8)),
            dma((8, 2)),
            dma((8, 2)),
            dma((2, 2)),
            dma((2, 2)),
            dma((2, 2)),
            dma((2, 2)),
            dma,
            dma,
        ],
        compiler_params=pltpu.CompilerParams(
            collective_id=0, has_side_effects=True, vmem_limit_bytes=60 * 2**20
        ),
        name="whole",
    )(*blocks, root, *updates, *pivots)
    return outs[0]


def shards(
    root_inverse,
    blocks_one,
    blocks_two,
    blocks_three,
    blocks_four,
    update_one,
    update_two,
    update_three,
    update_four,
    pivot_one,
    pivot_two,
    pivot_three,
    pivot_four,
):
    return whole(
        (blocks_one, blocks_two, blocks_three, blocks_four),
        root_inverse.reshape(8, BS, 2048),
        (update_one, update_two, update_three, update_four),
        (pivot_one, pivot_two, pivot_three, pivot_four),
    )


def solution(mesh):
    mesh = Mesh(mesh.devices.reshape(2, 2, 2, 2, 4, 2), AXES)
    leaf = AXES[:4]
    placed = (
        P(leaf, ("row", "col")),
        P(),
        P(),
        P(),
        P(),
        P("col", leaf),
        P("col", leaf),
        P("col", leaf),
        P("col", leaf),
        P("row", leaf),
        P("row", leaf),
        P("row", leaf),
        P("row", leaf),
    )
    return jax.shard_map(
        shards, mesh=mesh, in_specs=placed, out_specs=P(leaf, "row", "col"), check_vma=False
    )
```

```python
import jax
import jax.numpy as jnp
from jax import lax
from jax.experimental import pallas as pl
from jax.experimental.pallas import tpu as pltpu
from jax.sharding import Mesh, PartitionSpec as P

SEP = 1024
ANC = 2048
BS = 128
UNIT = 256
AXES = ("za", "zb", "ya", "yb", "row", "col")
MESH = pl.DeviceIdType.MESH
F32 = jnp.float32
BF16 = jnp.bfloat16


def place():
    z = lax.axis_index("za") * 2 + lax.axis_index("zb")
    y = lax.axis_index("ya") * 2 + lax.axis_index("yb")
    return z, y, lax.axis_index("row"), lax.axis_index("col")


def device(z, y, x, c):
    return (z // 2, z % 2, y // 2, y % 2, x, c)


def halves(value):
    high = value.astype(BF16)
    return high, (value - high.astype(F32)).astype(BF16)


def dot(a, b):
    return jnp.dot(a, b, preferred_element_type=F32)


def block_at(index, size):
    return pl.ds(pl.multiple_of(index * size, size), size)


def remote(src, dst, send, recv, to):
    return pltpu.make_async_remote_copy(
        src_ref=src, dst_ref=dst, send_sem=send, recv_sem=recv, device_id=to, device_id_type=MESH
    )


class Gather:
    def __init__(self, level, spot, u, v, ug, vg, sems):
        self.level, self.u, self.v, self.ug, self.vg = level, u, v, ug, vg
        self.z, self.y, self.x, self.c = spot
        self.own_sem, self.a_s, self.a_r, self.b_s, self.b_r, self.c_s, self.c_r, self.v_s, self.v_r = sems
        self.count = 8 >> level
        self.width = SEP // self.count
        self.me = lax.rem(self.z * 4 + self.y, self.count)
        self.first = self.x
        self.units = 1

    def peer(self, d):
        base = (self.z * 4 + self.y) // self.count * self.count
        return lax.rem(self.me + d, self.count), base

    def leaf(self, member, base):
        at = base + member
        return device(at // 4, lax.rem(at, 4), self.x, self.c)

    def cols(self, member):
        return block_at(member, self.width)

    def rows(self, first, units):
        return pl.ds(pl.multiple_of(first * UNIT, UNIT), units * UNIT)

    def load(self, buffer):
        return pltpu.make_async_copy(self.u, buffer, self.own_sem.at[0])

    def store(self, buffer):
        there = self.ug.at[self.c, :, self.cols(self.me)]
        return pltpu.make_async_copy(buffer, there, self.own_sem.at[0])

    def own_pivot(self):
        return pltpu.make_async_copy(
            self.v.at[block_at(self.c, BS), :], self.vg.at[:, self.cols(self.me)], self.own_sem.at[1]
        )

    def a_copy(self, d):
        member, base = self.peer(d)
        rows = self.rows(self.first, self.units)
        return remote(
            self.u.at[rows, :], self.ug.at[self.c, rows, self.cols(self.me)],
            self.a_s.at[d], self.a_r.at[self.me], self.leaf(member, base),
        )

    def v_copy(self, d):
        member, base = self.peer(d)
        return remote(
            self.v.at[block_at(self.c, BS), :], self.vg.at[:, self.cols(self.me)],
            self.v_s.at[d], self.v_r.at[self.me], self.leaf(member, base),
        )

    def a_arrived(self, member):
        rows = self.rows(self.first, self.units)
        there = self.ug.at[self.c, rows, self.cols(member)]
        return remote(there, there, self.a_s.at[0], self.a_r.at[member], device(self.z, self.y, self.x, 1 - self.c))

    def v_arrived(self, member):
        there = self.vg.at[:, self.cols(member)]
        return remote(there, there, self.v_s.at[0], self.v_r.at[member], device(self.z, self.y, self.x, 1 - self.c))

    def b_place(self, n, member, source):
        if n < 2:
            rows = self.rows(source, 1)
        else:
            unit = lax.rem(source + (3, 1)[n - 2], 4)
            rows = pl.ds(pl.multiple_of(unit * UNIT + (n - 2) * BS, BS), BS)
        return self.ug.at[self.c, rows, self.cols(member)]

    def b_copy(self, n, member):
        there = self.b_place(n, member, self.x)
        to = device(self.z, self.y, lax.rem(self.x + (1, 3)[n % 2], 4), self.c)
        return remote(there, there, self.b_s.at[n, member], self.b_r.at[n, member], to)

    def b_arrived(self, n, member):
        there = self.b_place(n, member, lax.rem(self.x + (3, 1)[n % 2], 4))
        return remote(
            there, there, self.b_s.at[n, member], self.b_r.at[n, member],
            device(self.z, self.y, self.x, 1 - self.c),
        )

    def c_copy(self, unit, half):
        there = self.ug.at[half, self.rows(unit, 1), :]
        return remote(
            there, there, self.c_s.at[unit], self.c_r.at[unit], device(self.z, self.y, self.x, 1 - self.c)
        )

    def begin(self, buffer):
        self.load(buffer).start()
        self.own_pivot().start()

    def send(self):
        for d in range(1, self.count):
            self.a_copy(d).start()

    def send_pivot(self):
        for d in range(1, self.count):
            self.v_copy(d).start()

    def others(self, body):
        def step(d, carry):
            body(lax.rem(self.me + self.count - d, self.count))
            return carry

        lax.fori_loop(1, self.count, step, 0)

    def share_out(self):
        def body(member):
            self.a_arrived(member).wait_recv()
            for n in range(2):
                self.b_copy(n, member).start()

        self.others(body)
        self.c_copy(self.x, self.c).start()

    def forward(self):
        def body(member):
            for n in range(2):
                self.b_arrived(n, member).wait_recv()
                self.b_copy(2 + n, member).start()

        self.others(body)
        for step in (3, 1):
            self.c_copy(lax.rem(self.x + step, 4), self.c).start()

    def collect(self):
        def body(member):
            for n in range(2, 4):
                self.b_arrived(n, member).wait_recv()

        self.others(body)
        self.c_copy(lax.rem(self.x + 2, 4), self.c).start()

    def collect_pivot(self):
        self.own_pivot().wait()

        def step(d, carry):
            self.v_arrived(lax.rem(self.me + self.count - d, self.count)).wait_recv()
            return carry

        lax.fori_loop(1, self.count, step, 0)

    def wait_other(self, unit):
        self.c_copy(unit, 1 - self.c).wait_recv()

    def finish(self):
        def step(d, carry):
            self.a_copy(d).wait_send()
            self.v_copy(d).wait_send()
            return carry

        lax.fori_loop(1, self.count, step, 0)

        def body(member):
            for n in range(4):
                self.b_copy(n, member).wait_send()

        self.others(body)
        for unit in range(4):
            self.c_copy(unit, self.c).wait_send()


def whole_kernel(
    one_ref, two_ref, three_ref, four_ref, root_ref, u1, u2, u3, u4, v1, v2, v3, v4,
    out_ref, ug1, ug3, ug4,
    core_in, mine, y_in, ready, held, hq0, hq1, pq0, pq1, ptl0, ptl1,
    u2v, u2hi, u2lo, uhi0, ulo0, stage, hs, st, vg, acc, sq, xin, outv,
    root_sem, core_s, core_r, ys, yr, h_s, h_r,
    own1, a1s, a1r, b1s, b1r, c1s, c1r, w1s, w1r,
    own3, a3s, a3r, b3s, b3r, c3s, c3r, w3s, w3r,
    c4s, c4r, v4_sem, u2_own, u2_s, u2_r, ag_s, ag_r, sg_s, sg_r,
    stage_sem, ps, pr, psr, prr, hx_s, hx_r, px_s, px_r, xs_s, xs_r, out_sem,
):
    spot = place()
    z, y, q, c = spot
    e = 2 * q + c
    partner = device(z, y, q, 1 - c)
    g1 = Gather(0, spot, u1, v1, ug1, vg.at[0], (own1, a1s, a1r, b1s, b1r, c1s, c1r, w1s, w1r))
    g3 = Gather(2, spot, u3, v3, ug3, vg.at[1], (own3, a3s, a3r, b3s, b3r, c3s, c3r, w3s, w3r))
    gathers = (g1, None, g3)
    leaf = z * 4 + y

    def peer(dy):
        return device(z, lax.rem(y + dy, 4), q, c)

    def picked_from(f, j, i):
        row = one_ref[f, 4 * z + i] - leaf * 8
        col = one_ref[f, 4 * q + j] - e * 16
        here = (row >= 0) & (row < 8) & (col >= 0) & (col < 16)
        return (
            jnp.minimum(jnp.maximum(col, 0), 15),
            jnp.minimum(jnp.maximum(row, 0), 7),
            jnp.where(here, 1.0, 0.0),
        )

    def chosen_block(depth, m):
        ids = (two_ref, three_ref, four_ref)[depth]
        quarter = m // 2
        block = ids[leaf // (4 >> depth), 4 * quarter + 2 + m % 2] - 6 * quarter - 2
        return jnp.minimum(jnp.maximum(block, 0), 3)

    def member_block(m, a):
        return 4 * (m // 2) + 2 * lax.rem(a, 2) + a // 2

    barrier = pltpu.get_barrier_semaphore()

    def signal(dev):
        pl.semaphore_signal(barrier, inc=1, device_id=dev, device_id_type=MESH)

    mine_f = z // 2

    def u2_own_copy():
        return pltpu.make_async_copy(u2, u2v.at[c], u2_own.at[0])

    def v2_own_copy():
        return pltpu.make_async_copy(v2.at[block_at(c, BS), :], sq.at[:, block_at(y, 256)], u2_own.at[1])

    def u2_push():
        return remote(u2, u2v.at[c], u2_s, u2_r, partner)

    def u4_push(unit):
        rows = pl.ds(unit * UNIT, UNIT)
        return remote(u4.at[rows, :], ug4.at[rows, :], c4s.at[unit], c4r.at[unit], partner)

    def v4_copy():
        return pltpu.make_async_copy(v4.at[block_at(c, BS), :], acc.at[1], v4_sem)

    travelling = (g1, g3)

    def enter(buffers):
        for g, buffer in zip(travelling, buffers):
            g.begin(buffer)
        u2_own_copy().start()
        v2_own_copy().start()
        for t in range(8):

            @pl.when(t != e)
            def _():
                signal(device(z, y, t // 2, t % 2))

        for d in range(1, 8):
            member, base = g1.peer(d)
            signal(g1.leaf(member, base))
        for p in range(4):
            for r in range(2):
                j = 2 * r + c

                @pl.when(jnp.logical_not((p == z) & (j == y) & (mine_f == c)))
                def _():
                    signal(device(p, j, q, mine_f))

        own = (mine_f == c) & (y % 2 == c)
        pl.semaphore_wait(barrier, jnp.where(own, 21, 22))

        g1.send()

        u2_push().start()

        for unit in range(4):
            u4_push(unit).start()
        v4_copy().start()

    def split_update(depth, uhi, ulo, start, stop):
        def unit_of(n):
            k = n // 2
            step = jnp.where(k == 0, 0, jnp.where(k == 1, 3, jnp.where(k == 2, 1, 2)))
            return lax.rem(q + step, 4), lax.rem(n + c, 2)

        def fetch(n, slot):
            unit, half = unit_of(n)
            rows = pl.ds(pl.multiple_of(unit * UNIT, UNIT), UNIT)
            if depth < 3:
                pltpu.make_async_copy(
                    gathers[depth].ug.at[half, rows, :], stage.at[slot], stage_sem.at[slot]
                ).start()
            else:

                @pl.when(half == c)
                def _():
                    pltpu.make_async_copy(u4.at[rows, :], stage.at[slot], stage_sem.at[slot]).start()

                @pl.when(half != c)
                def _():
                    pltpu.make_async_copy(ug4.at[rows, :], stage.at[slot], stage_sem.at[slot]).start()

        def arrived(n):
            unit, half = unit_of(n)

            @pl.when(half != c)
            def _():
                if depth < 3:
                    gathers[depth].wait_other(unit)
                else:
                    rows = pl.ds(pl.multiple_of(unit * UNIT, UNIT), UNIT)
                    remote(
                        ug4.at[rows, :], ug4.at[rows, :], c4s.at[unit], c4r.at[unit], partner
                    ).wait_recv()

        def step(n, carry):
            slot = lax.rem(n, 2)

            @pl.when(n + 1 < stop)
            def _():
                arrived(n + 1)
                fetch(n + 1, 1 - slot)

            pltpu.make_async_copy(
                u4.at[pl.ds(0, UNIT), :], stage.at[slot], stage_sem.at[slot]
            ).wait()
            unit, half = unit_of(n)
            for i in range(2):
                block = half * 8 + unit * 2 + i
                quarter, j = block // 4, lax.rem(block, 4)
                to = (2 * quarter + lax.rem(j, 2)) * 2 + j // 2
                hi, lo = halves(stage[slot, i * BS : i * BS + BS, :])
                uhi[block_at(to, BS), :] = hi
                ulo[block_at(to, BS), :] = lo
            return carry

        arrived(start)
        fetch(start, start % 2)
        lax.fori_loop(start, stop, step, 0)

    def take(rootv, picked, *buffers):
        def root_copy(j):
            return pltpu.make_async_copy(
                root_ref.at[:, :, j * BS : j * BS + BS], rootv.at[j], root_sem.at[j]
            )

        for j in range(16):
            root_copy(j).start()
        enter(buffers)
        for g, buffer in zip(travelling, buffers):
            g.load(buffer).wait()
            g.store(buffer).start()
        for j in range(16):
            root_copy(j).wait()

        def pick(n, carry):
            f, j = n // 4, n % 4
            for i in range(4):
                col, row, here = picked_from(f, j, i)
                picked[f, j, i % 2 * 2 + i // 2] = (rootv[col, row] * here).T
            return carry

        lax.fori_loop(0, 8, pick, 0)
        core = remote(picked.at[1 - c], core_in, core_s, core_r, partner)
        core.start()
        core.wait()
        mine[...] = picked[c] + core_in[...]
        for g, buffer in zip(travelling, buffers):
            g.store(buffer).wait()

    pl.run_scoped(
        take,
        pltpu.VMEM((16, 8, BS, BS), F32),
        pltpu.VMEM((2, 4, 4, BS, BS), F32),
        pltpu.VMEM((1024, 128), F32),
        pltpu.VMEM((1024, 512), F32),
    )

    def y_copy(d):
        to = lax.rem(y + d, 4)
        return remote(mine.at[to], y_in.at[d - 1], ys.at[d - 1], yr.at[d - 1], device(z, to, q, c))

    for d in (2, 1, 3):
        y_copy(d).start()
    g1.share_out()
    for d in (1, 3, 2):
        y_copy(d).wait()
    ready[...] = mine[y] + y_in[0] + y_in[1] + y_in[2]

    def h_copy(k, d):
        return remote(
            ready, held.at[y // 2, pl.ds(4 * z, 4)], h_s.at[k * 4 + d], h_r.at[z * 2 + y // 2],
            device(2 * c + k, lax.rem(y + d, 4), q, y % 2),
        )

    def to_self(k):
        return (2 * c + k == z) & (y % 2 == c)

    for d in (2, 1, 3):
        for k in range(2):
            h_copy(k, d).start()
    for k in range(2):

        @pl.when(jnp.logical_not(to_self(k)))
        def _():
            h_copy(k, 0).start()

        @pl.when(to_self(k))
        def _():
            held[y // 2, pl.ds(4 * z, 4)] = ready[...]

    u2_own_copy().wait()
    u2_push().wait()

    def split_two(b, carry):
        m = b // 2
        src = 4 * (m // 2) + 2 * lax.rem(b, 2) + lax.rem(m, 2)
        hi, lo = halves(u2v[src // 8, block_at(lax.rem(src, 8), BS), :])
        u2hi[block_at(b, BS), :] = hi
        u2lo[block_at(b, BS), :] = lo
        return carry

    lax.fori_loop(0, 16, split_two, 0)
    g1.forward()
    split_update(0, uhi0, ulo0, 0, 6)
    for p in range(4):
        for r in range(2):

            @pl.when(jnp.logical_not((p == z) & (2 * r + c == y) & (mine_f == c)))
            def _():
                there = held.at[r, pl.ds(4 * p, 4)]
                remote(there, there, h_s.at[0], h_r.at[p * 2 + r], partner).wait_recv()

    for d in (2, 1, 3):
        for k in range(2):
            h_copy(k, d).wait_send()
    for k in range(2):

        @pl.when(jnp.logical_not(to_self(k)))
        def _():
            h_copy(k, 0).wait_send()

    def pair_copy(ref, at, r, s_sem, r_sem):
        return remote(
            ref.at[2 * r + c], ref.at[2 * r + c], s_sem.at[at, r], r_sem.at[at, r], partner
        )

    def pair_arrived(ref, at, r, s_sem, r_sem):
        there = ref.at[2 * r + 1 - c]
        return remote(there, there, s_sem.at[at, r], r_sem.at[at, r], partner)

    def begin_level(at):
        hq = (hq0, hq1)[at]
        for r in range(2):
            for b in range(16):
                value = held[r, b]
                hi, lo = halves(value)
                hs[r * BS : r * BS + BS, b * BS : b * BS + BS] = hi
                hs[256 + r * BS : 256 + r * BS + BS, b * BS : b * BS + BS] = lo
                hq[2 * r + c, b] = value
            pair_copy(hq, at, r, hx_s, hx_r).start()

    def piece_copy(at, to):
        return remote(
            st.at[to], (ptl0, ptl1)[at].at[pl.ds(2 * e, 2)], ps.at[to], pr.at[at, e],
            device(z, y, to // 2, lax.rem(to, 2)),
        )

    def give(at, to, turned):
        ptl = (ptl0, ptl1)[at]

        @pl.when(to == e)
        def _():
            for r in range(2):
                ptl[2 * e + r] = turned[r]

        @pl.when(to != e)
        def _():
            for r in range(2):
                st[to, r] = turned[r]
            piece_copy(at, to).start()

    def part_copy(at, to, r):
        return remote(
            st.at[to, r], (ptl0, ptl1)[at].at[2 * e + r], psr.at[to, r], prr.at[e, r],
            device(z, y, to // 2, lax.rem(to, 2)),
        )

    def give_part(at, to, r, turned):
        ptl = (ptl0, ptl1)[at]

        @pl.when(to == e)
        def _():
            ptl[2 * e + r] = turned

        @pl.when(to != e)
        def _():
            st[to, r] = turned
            part_copy(at, to, r).start()

    def square_loop(at, out, cols, uhi, ulo, parts):
        ptl = (ptl0, ptl1)[at]

        def square_step(s, carry):
            k = s // 2
            step = jnp.where(k == 0, 0, jnp.where(k == 1, 1, jnp.where(k == 2, 3, 2)))
            m = 2 * lax.rem(q + step, 4) + lax.rem(s + c, 2)

            @pl.when(m != e)
            def _():
                if parts:
                    for r in range(2):
                        there = ptl.at[2 * m + r]
                        remote(there, there, psr.at[m, r], prr.at[m, r], partner).wait_recv()
                else:
                    there = ptl.at[pl.ds(2 * m, 2)]
                    remote(there, there, ps.at[m], pr.at[at, m], partner).wait_recv()

            hi, lo = halves(jnp.concatenate([ptl[2 * m], ptl[2 * m + 1]], 1))
            rows = block_at(m, 256)
            both = dot(jnp.concatenate([hi, lo], 0), uhi[rows, :])
            out[:, cols] += both[:BS] + both[BS:] + dot(hi, ulo[rows, :])
            return carry

        lax.fori_loop(0, 8, square_step, 0)

    def next_held(depth, at, square):
        hq, pq, ptl = ((hq0, pq0, ptl0), (hq1, pq1, ptl1))[at]
        for r in range(2):
            pair_arrived(hq, at, r, hx_s, hx_r).wait_recv()
            pair_arrived(pq, at, r, px_s, px_r).wait_recv()
        chosen = chosen_block(depth, e)
        for m in range(8):
            block = member_block(m, chosen_block(depth, m))
            held[0, 2 * m] = square[:, m * BS : m * BS + BS]
            held[0, 2 * m + 1] = -ptl[block]
            held[1, 2 * m] = -pq[chosen, :, m * BS : m * BS + BS]
            held[1, 2 * m + 1] = hq[chosen, block]

    def end_level(at, parts):
        hq, pq = ((hq0, pq0), (hq1, pq1))[at]
        for r in range(2):
            pair_copy(hq, at, r, hx_s, hx_r).wait_send()
            pair_copy(pq, at, r, px_s, px_r).wait_send()

        def sent(to, carry):
            @pl.when(to != e)
            def _():
                if parts:
                    for r in range(2):
                        part_copy(at, to, r).wait_send()
                else:
                    piece_copy(at, to).wait_send()

            return carry

        lax.fori_loop(0, 8, sent, 0)

    def level_two(later):
        pq = pq1
        begin_level(1)
        cols = block_at(y, 256)
        both = dot(hs[...], u2hi[...])
        part = both[:256] + both[256:] + dot(hs[:256, :], u2lo[...])

        def panel_out(dy, r):
            rows = pq.at[2 * r + c, :, cols]
            return remote(rows, rows, ag_s.at[dy, r], ag_r.at[y, r], peer(dy))

        def turn(m, r):
            for core in range(2):
                value = pq[2 * r + c, :, pl.ds(pl.multiple_of(m * 256 + core * BS, BS), BS)]
                give_part(1, 2 * m + core, r, value.T)

        for r in range(2):
            pq[2 * r + c, :, cols] = part[r * BS : r * BS + BS]
        for dy in (1, 3, 2):
            panel_out(dy, 0).start()
        turn(y, 0)
        turn(y, 1)
        for dy in (1, 3, 2):
            panel_out(dy, 0).wait_send()
        for dy in (1, 3, 2):
            panel_out(dy, 1).start()
        for r in range(2):
            for dy in (1, 3, 2):
                m = lax.rem(y + dy, 4)
                there = pq.at[2 * r + c, :, block_at(m, 256)]
                remote(there, there, ag_s.at[0, r], ag_r.at[m, r], partner).wait_recv()
                turn(m, r)
        for r in range(2):
            pair_copy(pq, 1, r, px_s, px_r).start()
        g3.forward()
        v2_own_copy().wait()
        square_loop(1, sq, cols, u2hi, u2lo, True)

        def square_out(dy):
            return remote(sq.at[:, cols], sq.at[:, cols], sg_s.at[dy], sg_r.at[y], peer(dy))

        for dy in (1, 3, 2):
            square_out(dy).start()
        later()
        for dy in (1, 3, 2):
            panel_out(dy, 1).wait_send()
            m = lax.rem(y + dy, 4)
            there = sq.at[:, block_at(m, 256)]
            remote(there, there, sg_s.at[0], sg_r.at[m], partner).wait_recv()
        next_held(1, 1, sq)
        for dy in (1, 3, 2):
            square_out(dy).wait_send()
        end_level(1, True)

    def out_copy(first, rows):
        return pltpu.make_async_copy(
            outv.at[pl.ds(first, rows), :], out_ref.at[0, pl.ds(first, rows), :], out_sem.at[min(first, 1)]
        )

    def level(depth, uhi, ulo, early, meanwhile):
        last = depth == 3
        at = depth % 2
        hq, pq, ptl = ((hq0, pq0, ptl0), (hq1, pq1, ptl1))[at]
        begin_level(at)
        early()

        def panel_step(k, carry):
            step = jnp.where(k == 0, 2, jnp.where(k == 1, 1, jnp.where(k == 2, 3, 0)))
            t = lax.rem(q + step, 4)
            cols = block_at(t, 256)
            both = dot(hs[...], uhi[:, cols])
            part = both[:256] + both[256:] + dot(hs[:256, :], ulo[:, cols])
            for r in range(2):
                pq[2 * r + c, :, cols] = part[r * BS : r * BS + BS]
            for core in range(2):
                turned = [
                    part[r * BS : r * BS + BS, core * BS : core * BS + BS].T for r in range(2)
                ]
                give(at, 2 * t + core, turned)
            return carry

        lax.fori_loop(0, 4, panel_step, 0)
        for r in range(2):
            pair_copy(pq, at, r, px_s, px_r).start()
        meanwhile()
        if last:
            v4_copy().wait()
            acc[0] = acc[1]
            for r in range(2):
                pair_arrived(hq, at, r, hx_s, hx_r).wait_recv()
                pair_arrived(pq, at, r, px_s, px_r).wait_recv()
            for a in range(4):
                rows = slice(256 + a * BS, 256 + a * BS + BS)
                for p in range(2):
                    quarter = 2 * c + p
                    outv[rows, p * 768 : p * 768 + 256] = -pq[a, :, block_at(quarter, 256)]
                    for b in range(4):
                        block = 2 * (2 * quarter + b % 2) + b // 2
                        to = p * 768 + 256 + b * BS
                        outv[rows, to : to + BS] = hq[a, block]
            out_copy(256, 512).start()
        else:
            gathers[depth].collect_pivot()
            acc[0] = vg[depth // 2]
        square_loop(at, acc.at[0], slice(None), uhi, ulo, False)
        if not last:
            next_held(depth, at, acc.at[0])
        else:

            def rows_of(half):
                for p in range(2):
                    quarter = 2 * half + p
                    yield p * 768, acc[0, :, block_at(quarter, 256)]
                    for a in range(4):
                        yield p * 768 + 256 + a * BS, -ptl[2 * (2 * quarter + a % 2) + a // 2]

            for to, value in rows_of(1 - c):
                xin[1, :, to : to + value.shape[1]] = value
            cross = remote(xin.at[1], xin.at[0], xs_s, xs_r, partner)
            cross.start()
            for to, value in rows_of(c):
                outv[block_at(c, BS), to : to + value.shape[1]] = value
            cross.wait()
            outv[block_at(1 - c, BS), :] = xin[0]
            out_copy(0, 256).start()
            out_copy(0, 256).wait()
            out_copy(256, 512).wait()

        end_level(at, False)

    def levels(uhi1, ulo1):
        def rest_of_one():
            g1.collect()
            split_update(0, uhi0, ulo0, 6, 8)

        def three():
            g3.collect()
            split_update(2, uhi1, ulo1, 0, 8)

        g1.send_pivot()
        g3.send()
        g3.send_pivot()
        level(0, uhi0, ulo0, rest_of_one, lambda: None)
        g3.share_out()
        level_two(three)
        level(2, uhi1, ulo1, lambda: None, lambda: split_update(3, uhi0, ulo0, 0, 8))
        level(3, uhi0, ulo0, lambda: None, lambda: None)

    pl.run_scoped(levels, pltpu.VMEM((ANC, SEP), BF16), pltpu.VMEM((ANC, SEP), BF16))
    g1.finish()
    g3.finish()
    for unit in range(4):
        u4_push(unit).wait_send()


def whole(blocks, root, updates, pivots):
    dma = pltpu.SemaphoreType.DMA
    any_space = pl.BlockSpec(memory_space=pl.ANY)
    smem = pl.BlockSpec(memory_space=pltpu.SMEM)
    gather_sems = []
    for n in (8, 2):
        gather_sems += [
            dma((2,)), dma((n,)), dma((n,)), dma((4, n)), dma((4, n)), dma((4,)), dma((4,)), dma((n,)), dma((n,)),
        ]
    outs = pl.pallas_call(
        whole_kernel,
        out_shape=[jax.ShapeDtypeStruct((1, 768, 1536), F32)]
        + [jax.ShapeDtypeStruct((2, 1024, 1024), F32)] * 2
        + [jax.ShapeDtypeStruct((1024, 1024), F32)],
        in_specs=[smem] * 4 + [any_space] * 9,
        out_specs=[any_space] * 4,
        scratch_shapes=[
            pltpu.VMEM((4, 4, BS, BS), F32),
            pltpu.VMEM((4, 4, BS, BS), F32),
            pltpu.VMEM((3, 4, BS, BS), F32),
            pltpu.VMEM((4, BS, BS), F32),
            pltpu.VMEM((2, 16, BS, BS), F32),
            pltpu.VMEM((4, 16, BS, BS), F32),
            pltpu.VMEM((4, 16, BS, BS), F32),
            pltpu.VMEM((4, BS, SEP), F32),
            pltpu.VMEM((4, BS, SEP), F32),
            pltpu.VMEM((16, BS, BS), F32),
            pltpu.VMEM((16, BS, BS), F32),
            pltpu.VMEM((2, 1024, 256), F32),
            pltpu.VMEM((ANC, 256), BF16),
            pltpu.VMEM((ANC, 256), BF16),
            pltpu.VMEM((ANC, SEP), BF16),
            pltpu.VMEM((ANC, SEP), BF16),
            pltpu.VMEM((2, UNIT, SEP), F32),
            pltpu.VMEM((512, ANC), BF16),
            pltpu.VMEM((8, 2, BS, BS), F32),
            pltpu.VMEM((2, BS, SEP), F32),
            pltpu.VMEM((2, BS, SEP), F32),
            pltpu.VMEM((BS, SEP), F32),
            pltpu.VMEM((2, BS, 1536), F32),
            pltpu.VMEM((768, 1536), F32),
            dma((16,)),
            dma,
            dma,
            dma((3,)),
            dma((3,)),
            dma((8,)),
            dma((8,)),
        ]
        + gather_sems
        + [
            dma((4,)),
            dma((4,)),
            dma,
            dma((2,)),
            dma,
            dma,
            dma((4, 2)),
            dma((4, 2)),
            dma((4,)),
            dma((4,)),
            dma((2,)),
            dma((8,)),
            dma((2, 8)),
            dma((8, 2)),
            dma((8, 2)),
            dma((2, 2)),
            dma((2, 2)),
            dma((2, 2)),
            dma((2, 2)),
            dma,
            dma,
            dma((2,)),
        ],
        compiler_params=pltpu.CompilerParams(
            collective_id=0, has_side_effects=True, vmem_limit_bytes=60 * 2**20
        ),
        name="whole",
    )(*blocks, root, *updates, *pivots)
    return outs[0]


def shards(
    root_inverse,
    blocks_one,
    blocks_two,
    blocks_three,
    blocks_four,
    update_one,
    update_two,
    update_three,
    update_four,
    pivot_one,
    pivot_two,
    pivot_three,
    pivot_four,
):
    return whole(
        (blocks_one, blocks_two, blocks_three, blocks_four),
        root_inverse.reshape(8, BS, 2048),
        (update_one, update_two, update_three, update_four),
        (pivot_one, pivot_two, pivot_three, pivot_four),
    )


def solution(mesh):
    mesh = Mesh(mesh.devices.reshape(2, 2, 2, 2, 4, 2), AXES)
    leaf = AXES[:4]
    placed = (
        P(leaf, ("row", "col")),
        P(),
        P(),
        P(),
        P(),
        P("col", leaf),
        P("col", leaf),
        P("col", leaf),
        P("col", leaf),
        P("row", leaf),
        P("row", leaf),
        P("row", leaf),
        P("row", leaf),
    )
    return jax.shard_map(
        shards, mesh=mesh, in_specs=placed, out_specs=P(leaf, "row", "col"), check_vma=False
    )
```

```python
import jax
import jax.numpy as jnp
from jax import lax
from jax.experimental import pallas as pl
from jax.experimental.pallas import tpu as pltpu
from jax.sharding import Mesh, PartitionSpec as P

SEP = 1024
ANC = 2048
BS = 128
UNIT = 256
AXES = ("za", "zb", "ya", "yb", "row", "col")
MESH = pl.DeviceIdType.MESH
F32 = jnp.float32
BF16 = jnp.bfloat16


def place():
    z = lax.axis_index("za") * 2 + lax.axis_index("zb")
    y = lax.axis_index("ya") * 2 + lax.axis_index("yb")
    return z, y, lax.axis_index("row"), lax.axis_index("col")


def device(z, y, x, c):
    return (z // 2, z % 2, y // 2, y % 2, x, c)


def halves(value):
    high = value.astype(BF16)
    return high, (value - high.astype(F32)).astype(BF16)


def dot(a, b):
    return jnp.dot(a, b, preferred_element_type=F32)


def block_at(index, size):
    return pl.ds(pl.multiple_of(index * size, size), size)


def remote(src, dst, send, recv, to):
    return pltpu.make_async_remote_copy(
        src_ref=src, dst_ref=dst, send_sem=send, recv_sem=recv, device_id=to, device_id_type=MESH
    )


class Gather:
    def __init__(self, level, spot, u, v, ug, vg, sems):
        self.level, self.u, self.v, self.ug, self.vg = level, u, v, ug, vg
        self.z, self.y, self.x, self.c = spot
        self.own_sem, self.a_s, self.a_r, self.b_s, self.b_r, self.c_s, self.c_r, self.v_s, self.v_r = sems
        self.count = 8 >> level
        self.width = SEP // self.count
        self.me = lax.rem(self.z * 4 + self.y, self.count)
        self.first = self.x
        self.units = 1

    def peer(self, d):
        base = (self.z * 4 + self.y) // self.count * self.count
        return lax.rem(self.me + d, self.count), base

    def leaf(self, member, base):
        at = base + member
        return device(at // 4, lax.rem(at, 4), self.x, self.c)

    def cols(self, member):
        return block_at(member, self.width)

    def rows(self, first, units):
        return pl.ds(pl.multiple_of(first * UNIT, UNIT), units * UNIT)

    def load(self, buffer):
        return pltpu.make_async_copy(self.u, buffer, self.own_sem.at[0])

    def store(self, buffer):
        there = self.ug.at[self.c, :, self.cols(self.me)]
        return pltpu.make_async_copy(buffer, there, self.own_sem.at[0])

    def own_pivot(self):
        return pltpu.make_async_copy(
            self.v.at[block_at(self.c, BS), :], self.vg.at[:, self.cols(self.me)], self.own_sem.at[1]
        )

    def a_copy(self, d):
        member, base = self.peer(d)
        rows = self.rows(self.first, self.units)
        return remote(
            self.u.at[rows, :], self.ug.at[self.c, rows, self.cols(self.me)],
            self.a_s.at[d], self.a_r.at[self.me], self.leaf(member, base),
        )

    def v_copy(self, d):
        member, base = self.peer(d)
        return remote(
            self.v.at[block_at(self.c, BS), :], self.vg.at[:, self.cols(self.me)],
            self.v_s.at[d], self.v_r.at[self.me], self.leaf(member, base),
        )

    def a_arrived(self, member):
        rows = self.rows(self.first, self.units)
        there = self.ug.at[self.c, rows, self.cols(member)]
        return remote(there, there, self.a_s.at[0], self.a_r.at[member], device(self.z, self.y, self.x, 1 - self.c))

    def v_arrived(self, member):
        there = self.vg.at[:, self.cols(member)]
        return remote(there, there, self.v_s.at[0], self.v_r.at[member], device(self.z, self.y, self.x, 1 - self.c))

    def b_place(self, n, member, source):
        if n < 2:
            rows = self.rows(source, 1)
        else:
            unit = lax.rem(source + (3, 1)[n - 2], 4)
            rows = pl.ds(pl.multiple_of(unit * UNIT + (n - 2) * BS, BS), BS)
        return self.ug.at[self.c, rows, self.cols(member)]

    def b_copy(self, n, member):
        there = self.b_place(n, member, self.x)
        to = device(self.z, self.y, lax.rem(self.x + (1, 3)[n % 2], 4), self.c)
        return remote(there, there, self.b_s.at[n, member], self.b_r.at[n, member], to)

    def b_arrived(self, n, member):
        there = self.b_place(n, member, lax.rem(self.x + (3, 1)[n % 2], 4))
        return remote(
            there, there, self.b_s.at[n, member], self.b_r.at[n, member],
            device(self.z, self.y, self.x, 1 - self.c),
        )

    def c_copy(self, unit, half):
        there = self.ug.at[half, self.rows(unit, 1), :]
        return remote(
            there, there, self.c_s.at[unit], self.c_r.at[unit], device(self.z, self.y, self.x, 1 - self.c)
        )

    def begin(self, buffer):
        self.load(buffer).start()
        self.own_pivot().start()

    def send(self):
        for d in range(1, self.count):
            self.a_copy(d).start()

    def send_pivot(self):
        for d in range(1, self.count):
            self.v_copy(d).start()

    def others(self, body):
        def step(d, carry):
            body(lax.rem(self.me + self.count - d, self.count))
            return carry

        lax.fori_loop(1, self.count, step, 0)

    def share_out(self):
        def body(member):
            self.a_arrived(member).wait_recv()
            for n in range(2):
                self.b_copy(n, member).start()

        self.others(body)
        self.c_copy(self.x, self.c).start()

    def forward(self):
        def body(member):
            for n in range(2):
                self.b_arrived(n, member).wait_recv()
                self.b_copy(2 + n, member).start()

        self.others(body)
        for step in (3, 1):
            self.c_copy(lax.rem(self.x + step, 4), self.c).start()

    def collect(self):
        def body(member):
            for n in range(2, 4):
                self.b_arrived(n, member).wait_recv()

        self.others(body)
        self.c_copy(lax.rem(self.x + 2, 4), self.c).start()

    def collect_pivot(self):
        self.own_pivot().wait()

        def step(d, carry):
            self.v_arrived(lax.rem(self.me + self.count - d, self.count)).wait_recv()
            return carry

        lax.fori_loop(1, self.count, step, 0)

    def wait_other(self, unit):
        self.c_copy(unit, 1 - self.c).wait_recv()

    def finish(self):
        def step(d, carry):
            self.a_copy(d).wait_send()
            self.v_copy(d).wait_send()
            return carry

        lax.fori_loop(1, self.count, step, 0)

        def body(member):
            for n in range(4):
                self.b_copy(n, member).wait_send()

        self.others(body)
        for unit in range(4):
            self.c_copy(unit, self.c).wait_send()


def whole_kernel(
    one_ref, two_ref, three_ref, four_ref, root_ref, u1, u2, u3, u4, v1, v2, v3, v4,
    out_ref, ug1, ug3, ug4,
    core_in, mine, y_in, ready, held, hq0, hq1, pq0, pq1, ptl0, ptl1,
    u2v, u2hi, u2lo, uhi0, ulo0, stage, hs, st, vg, acc, sq, xin, outv,
    root_sem, core_s, core_r, ys, yr, h_s, h_r,
    own1, a1s, a1r, b1s, b1r, c1s, c1r, w1s, w1r,
    own3, a3s, a3r, b3s, b3r, c3s, c3r, w3s, w3r,
    c4s, c4r, v4_sem, u2_own, u2_s, u2_r, ag_s, ag_r, sg_s, sg_r,
    stage_sem, ps, pr, psr, prr, hx_s, hx_r, px_s, px_r, xs_s, xs_r, out_sem,
):
    spot = place()
    z, y, q, c = spot
    e = 2 * q + c
    partner = device(z, y, q, 1 - c)
    g1 = Gather(0, spot, u1, v1, ug1, vg.at[0], (own1, a1s, a1r, b1s, b1r, c1s, c1r, w1s, w1r))
    g3 = Gather(2, spot, u3, v3, ug3, vg.at[1], (own3, a3s, a3r, b3s, b3r, c3s, c3r, w3s, w3r))
    gathers = (g1, None, g3)
    leaf = z * 4 + y

    def peer(dy):
        return device(z, lax.rem(y + dy, 4), q, c)

    def picked_from(f, j, i):
        row = one_ref[f, 4 * z + i] - leaf * 8
        col = one_ref[f, 4 * q + j] - e * 16
        here = (row >= 0) & (row < 8) & (col >= 0) & (col < 16)
        return (
            jnp.minimum(jnp.maximum(col, 0), 15),
            jnp.minimum(jnp.maximum(row, 0), 7),
            jnp.where(here, 1.0, 0.0),
        )

    def chosen_block(depth, m):
        ids = (two_ref, three_ref, four_ref)[depth]
        quarter = m // 2
        block = ids[leaf // (4 >> depth), 4 * quarter + 2 + m % 2] - 6 * quarter - 2
        return jnp.minimum(jnp.maximum(block, 0), 3)

    def member_block(m, a):
        return 4 * (m // 2) + 2 * lax.rem(a, 2) + a // 2

    barrier = pltpu.get_barrier_semaphore()

    def signal(dev):
        pl.semaphore_signal(barrier, inc=1, device_id=dev, device_id_type=MESH)

    mine_f = z // 2

    def u2_own_copy():
        return pltpu.make_async_copy(u2, u2v.at[c], u2_own.at[0])

    def v2_own_copy():
        return pltpu.make_async_copy(v2.at[block_at(c, BS), :], sq.at[:, block_at(y, 256)], u2_own.at[1])

    def u2_push():
        return remote(u2, u2v.at[c], u2_s, u2_r, partner)

    def u4_push(unit):
        rows = pl.ds(unit * UNIT, UNIT)
        return remote(u4.at[rows, :], ug4.at[rows, :], c4s.at[unit], c4r.at[unit], partner)

    def v4_copy():
        return pltpu.make_async_copy(v4.at[block_at(c, BS), :], acc.at[1], v4_sem)

    travelling = (g1, g3)

    def enter(buffers):
        for g, buffer in zip(travelling, buffers):
            g.begin(buffer)
        u2_own_copy().start()
        v2_own_copy().start()
        for t in range(8):

            @pl.when(t != e)
            def _():
                signal(device(z, y, t // 2, t % 2))

        for d in range(1, 8):
            member, base = g1.peer(d)
            signal(g1.leaf(member, base))
        for p in range(4):
            for r in range(2):
                j = 2 * r + c

                @pl.when(jnp.logical_not((p == z) & (j == y) & (mine_f == c)))
                def _():
                    signal(device(p, j, q, mine_f))

        own = (mine_f == c) & (y % 2 == c)
        pl.semaphore_wait(barrier, jnp.where(own, 21, 22))

        g1.send()

        u2_push().start()

        for unit in range(4):
            u4_push(unit).start()
        v4_copy().start()

    def split_update(depth, uhi, ulo, start, stop):
        def unit_of(n):
            k = n // 2
            step = jnp.where(k == 0, 0, jnp.where(k == 1, 3, jnp.where(k == 2, 1, 2)))
            return lax.rem(q + step, 4), lax.rem(n + c, 2)

        def fetch(n, slot):
            unit, half = unit_of(n)
            rows = pl.ds(pl.multiple_of(unit * UNIT, UNIT), UNIT)
            if depth < 3:
                pltpu.make_async_copy(
                    gathers[depth].ug.at[half, rows, :], stage.at[slot], stage_sem.at[slot]
                ).start()
            else:

                @pl.when(half == c)
                def _():
                    pltpu.make_async_copy(u4.at[rows, :], stage.at[slot], stage_sem.at[slot]).start()

                @pl.when(half != c)
                def _():
                    pltpu.make_async_copy(ug4.at[rows, :], stage.at[slot], stage_sem.at[slot]).start()

        def arrived(n):
            unit, half = unit_of(n)

            @pl.when(half != c)
            def _():
                if depth < 3:
                    gathers[depth].wait_other(unit)
                else:
                    rows = pl.ds(pl.multiple_of(unit * UNIT, UNIT), UNIT)
                    remote(
                        ug4.at[rows, :], ug4.at[rows, :], c4s.at[unit], c4r.at[unit], partner
                    ).wait_recv()

        def step(n, carry):
            slot = lax.rem(n, 2)

            @pl.when(n + 1 < stop)
            def _():
                arrived(n + 1)
                fetch(n + 1, 1 - slot)

            pltpu.make_async_copy(
                u4.at[pl.ds(0, UNIT), :], stage.at[slot], stage_sem.at[slot]
            ).wait()
            unit, half = unit_of(n)
            for i in range(2):
                block = half * 8 + unit * 2 + i
                quarter, j = block // 4, lax.rem(block, 4)
                to = (2 * quarter + lax.rem(j, 2)) * 2 + j // 2
                hi, lo = halves(stage[slot, i * BS : i * BS + BS, :])
                uhi[block_at(to, BS), :] = hi
                ulo[block_at(to, BS), :] = lo
            return carry

        arrived(start)
        fetch(start, start % 2)
        lax.fori_loop(start, stop, step, 0)

    def take(rootv, picked, *buffers):
        def root_copy(j):
            return pltpu.make_async_copy(
                root_ref.at[:, :, j * BS : j * BS + BS], rootv.at[j], root_sem.at[j]
            )

        for j in range(16):
            root_copy(j).start()
        enter(buffers)
        for g, buffer in zip(travelling, buffers):
            g.load(buffer).wait()
            g.store(buffer).start()
        for j in range(16):
            root_copy(j).wait()

        def pick(n, carry):
            f, j = n // 4, n % 4
            for i in range(4):
                col, row, here = picked_from(f, j, i)
                picked[f, j, i % 2 * 2 + i // 2] = (rootv[col, row] * here).T
            return carry

        lax.fori_loop(0, 8, pick, 0)
        core = remote(picked.at[1 - c], core_in, core_s, core_r, partner)
        core.start()
        core.wait()
        mine[...] = picked[c] + core_in[...]
        for g, buffer in zip(travelling, buffers):
            g.store(buffer).wait()

    pl.run_scoped(
        take,
        pltpu.VMEM((16, 8, BS, BS), F32),
        pltpu.VMEM((2, 4, 4, BS, BS), F32),
        pltpu.VMEM((1024, 128), F32),
        pltpu.VMEM((1024, 512), F32),
    )

    def y_copy(d):
        to = lax.rem(y + d, 4)
        return remote(mine.at[to], y_in.at[d - 1], ys.at[d - 1], yr.at[d - 1], device(z, to, q, c))

    for d in (2, 1, 3):
        y_copy(d).start()
    g1.share_out()
    for d in (1, 3, 2):
        y_copy(d).wait()
    ready[...] = mine[y] + y_in[0] + y_in[1] + y_in[2]

    def h_copy(k, d):
        return remote(
            ready, held.at[y // 2, pl.ds(4 * z, 4)], h_s.at[k * 4 + d], h_r.at[z * 2 + y // 2],
            device(2 * c + k, lax.rem(y + d, 4), q, y % 2),
        )

    def to_self(k):
        return (2 * c + k == z) & (y % 2 == c)

    for d in (2, 1, 3):
        for k in range(2):
            h_copy(k, d).start()
    for k in range(2):

        @pl.when(jnp.logical_not(to_self(k)))
        def _():
            h_copy(k, 0).start()

        @pl.when(to_self(k))
        def _():
            held[y // 2, pl.ds(4 * z, 4)] = ready[...]

    u2_own_copy().wait()
    u2_push().wait()

    def split_two(b, carry):
        m = b // 2
        src = 4 * (m // 2) + 2 * lax.rem(b, 2) + lax.rem(m, 2)
        hi, lo = halves(u2v[src // 8, block_at(lax.rem(src, 8), BS), :])
        u2hi[block_at(b, BS), :] = hi
        u2lo[block_at(b, BS), :] = lo
        return carry

    lax.fori_loop(0, 16, split_two, 0)
    g1.forward()
    split_update(0, uhi0, ulo0, 0, 6)
    for p in range(4):
        for r in range(2):

            @pl.when(jnp.logical_not((p == z) & (2 * r + c == y) & (mine_f == c)))
            def _():
                there = held.at[r, pl.ds(4 * p, 4)]
                remote(there, there, h_s.at[0], h_r.at[p * 2 + r], partner).wait_recv()

    def pair_copy(ref, at, r, s_sem, r_sem):
        return remote(
            ref.at[2 * r + c], ref.at[2 * r + c], s_sem.at[at, r], r_sem.at[at, r], partner
        )

    def pair_arrived(ref, at, r, s_sem, r_sem):
        there = ref.at[2 * r + 1 - c]
        return remote(there, there, s_sem.at[at, r], r_sem.at[at, r], partner)

    def begin_level(at):
        hq = (hq0, hq1)[at]
        for r in range(2):
            for b in range(16):
                value = held[r, b]
                hi, lo = halves(value)
                hs[r * BS : r * BS + BS, b * BS : b * BS + BS] = hi
                hs[256 + r * BS : 256 + r * BS + BS, b * BS : b * BS + BS] = lo
                hq[2 * r + c, b] = value
            pair_copy(hq, at, r, hx_s, hx_r).start()

    def piece_copy(at, to):
        return remote(
            st.at[to], (ptl0, ptl1)[at].at[pl.ds(2 * e, 2)], ps.at[to], pr.at[at, e],
            device(z, y, to // 2, lax.rem(to, 2)),
        )

    def give(at, to, turned):
        ptl = (ptl0, ptl1)[at]

        @pl.when(to == e)
        def _():
            for r in range(2):
                ptl[2 * e + r] = turned[r]

        @pl.when(to != e)
        def _():
            for r in range(2):
                st[to, r] = turned[r]
            piece_copy(at, to).start()

    def part_copy(at, to, r):
        return remote(
            st.at[to, r], (ptl0, ptl1)[at].at[2 * e + r], psr.at[to, r], prr.at[e, r],
            device(z, y, to // 2, lax.rem(to, 2)),
        )

    def give_part(at, to, r, turned):
        ptl = (ptl0, ptl1)[at]

        @pl.when(to == e)
        def _():
            ptl[2 * e + r] = turned

        @pl.when(to != e)
        def _():
            st[to, r] = turned
            part_copy(at, to, r).start()

    def square_loop(at, out, cols, uhi, ulo, parts):
        ptl = (ptl0, ptl1)[at]

        def square_step(s, carry):
            k = s // 2
            step = jnp.where(k == 0, 0, jnp.where(k == 1, 1, jnp.where(k == 2, 3, 2)))
            m = 2 * lax.rem(q + step, 4) + lax.rem(s + c, 2)

            @pl.when(m != e)
            def _():
                if parts:
                    for r in range(2):
                        there = ptl.at[2 * m + r]
                        remote(there, there, psr.at[m, r], prr.at[m, r], partner).wait_recv()
                else:
                    there = ptl.at[pl.ds(2 * m, 2)]
                    remote(there, there, ps.at[m], pr.at[at, m], partner).wait_recv()

            hi, lo = halves(jnp.concatenate([ptl[2 * m], ptl[2 * m + 1]], 1))
            rows = block_at(m, 256)
            both = dot(jnp.concatenate([hi, lo], 0), uhi[rows, :])
            out[:, cols] += both[:BS] + both[BS:] + dot(hi, ulo[rows, :])
            return carry

        lax.fori_loop(0, 8, square_step, 0)

    def next_held(depth, at, square):
        hq, pq, ptl = ((hq0, pq0, ptl0), (hq1, pq1, ptl1))[at]
        for r in range(2):
            pair_arrived(hq, at, r, hx_s, hx_r).wait_recv()
            pair_arrived(pq, at, r, px_s, px_r).wait_recv()
        chosen = chosen_block(depth, e)
        for m in range(8):
            block = member_block(m, chosen_block(depth, m))
            held[0, 2 * m] = square[:, m * BS : m * BS + BS]
            held[0, 2 * m + 1] = -ptl[block]
            held[1, 2 * m] = -pq[chosen, :, m * BS : m * BS + BS]
            held[1, 2 * m + 1] = hq[chosen, block]

    def end_level(at, parts):
        hq, pq = ((hq0, pq0), (hq1, pq1))[at]
        for r in range(2):
            pair_copy(hq, at, r, hx_s, hx_r).wait_send()
            pair_copy(pq, at, r, px_s, px_r).wait_send()

        def sent(to, carry):
            @pl.when(to != e)
            def _():
                if parts:
                    for r in range(2):
                        part_copy(at, to, r).wait_send()
                else:
                    piece_copy(at, to).wait_send()

            return carry

        lax.fori_loop(0, 8, sent, 0)

    def level_two(later):
        pq = pq1
        begin_level(1)
        cols = block_at(y, 256)
        both = dot(hs[...], u2hi[...])
        part = both[:256] + both[256:] + dot(hs[:256, :], u2lo[...])

        def panel_out(dy, r):
            rows = pq.at[2 * r + c, :, cols]
            return remote(rows, rows, ag_s.at[dy, r], ag_r.at[y, r], peer(dy))

        def turn(m, r):
            for core in range(2):
                value = pq[2 * r + c, :, pl.ds(pl.multiple_of(m * 256 + core * BS, BS), BS)]
                give_part(1, 2 * m + core, r, value.T)

        for r in range(2):
            pq[2 * r + c, :, cols] = part[r * BS : r * BS + BS]
        for dy in (1, 3, 2):
            panel_out(dy, 0).start()
        turn(y, 0)
        turn(y, 1)
        for dy in (1, 3, 2):
            panel_out(dy, 0).wait_send()
        for dy in (1, 3, 2):
            panel_out(dy, 1).start()
        for r in range(2):
            for dy in (1, 3, 2):
                m = lax.rem(y + dy, 4)
                there = pq.at[2 * r + c, :, block_at(m, 256)]
                remote(there, there, ag_s.at[0, r], ag_r.at[m, r], partner).wait_recv()
                turn(m, r)
        for r in range(2):
            pair_copy(pq, 1, r, px_s, px_r).start()
        g3.forward()
        v2_own_copy().wait()
        square_loop(1, sq, cols, u2hi, u2lo, True)

        def square_out(dy):
            return remote(sq.at[:, cols], sq.at[:, cols], sg_s.at[dy], sg_r.at[y], peer(dy))

        for dy in (1, 3, 2):
            square_out(dy).start()
        later()
        for dy in (1, 3, 2):
            panel_out(dy, 1).wait_send()
            m = lax.rem(y + dy, 4)
            there = sq.at[:, block_at(m, 256)]
            remote(there, there, sg_s.at[0], sg_r.at[m], partner).wait_recv()
        next_held(1, 1, sq)
        for dy in (1, 3, 2):
            square_out(dy).wait_send()
        end_level(1, True)

    def out_copy(first, rows):
        return pltpu.make_async_copy(
            outv.at[pl.ds(first, rows), :], out_ref.at[0, pl.ds(first, rows), :], out_sem.at[min(first, 1)]
        )

    def level(depth, uhi, ulo, early, meanwhile):
        last = depth == 3
        at = depth % 2
        hq, pq, ptl = ((hq0, pq0, ptl0), (hq1, pq1, ptl1))[at]
        begin_level(at)
        early()

        def panel_step(k, carry):
            step = jnp.where(k == 0, 2, jnp.where(k == 1, 1, jnp.where(k == 2, 3, 0)))
            t = lax.rem(q + step, 4)
            cols = block_at(t, 256)
            both = dot(hs[...], uhi[:, cols])
            part = both[:256] + both[256:] + dot(hs[:256, :], ulo[:, cols])
            for r in range(2):
                pq[2 * r + c, :, cols] = part[r * BS : r * BS + BS]
            for core in range(2):
                turned = [
                    part[r * BS : r * BS + BS, core * BS : core * BS + BS].T for r in range(2)
                ]
                give(at, 2 * t + core, turned)
            return carry

        lax.fori_loop(0, 4, panel_step, 0)
        for r in range(2):
            pair_copy(pq, at, r, px_s, px_r).start()
        meanwhile()
        if last:
            v4_copy().wait()
            acc[0] = acc[1]
            for r in range(2):
                pair_arrived(hq, at, r, hx_s, hx_r).wait_recv()
                pair_arrived(pq, at, r, px_s, px_r).wait_recv()
            for a in range(4):
                rows = slice(256 + a * BS, 256 + a * BS + BS)
                for p in range(2):
                    quarter = 2 * c + p
                    outv[rows, p * 768 : p * 768 + 256] = -pq[a, :, block_at(quarter, 256)]
                    for b in range(4):
                        block = 2 * (2 * quarter + b % 2) + b // 2
                        to = p * 768 + 256 + b * BS
                        outv[rows, to : to + BS] = hq[a, block]
            out_copy(256, 512).start()
        else:
            gathers[depth].collect_pivot()
            acc[0] = vg[depth // 2]
        square_loop(at, acc.at[0], slice(None), uhi, ulo, False)
        if not last:
            next_held(depth, at, acc.at[0])
        else:

            def rows_of(half):
                for p in range(2):
                    quarter = 2 * half + p
                    yield p * 768, acc[0, :, block_at(quarter, 256)]
                    for a in range(4):
                        yield p * 768 + 256 + a * BS, -ptl[2 * (2 * quarter + a % 2) + a // 2]

            for to, value in rows_of(1 - c):
                xin[1, :, to : to + value.shape[1]] = value
            cross = remote(xin.at[1], xin.at[0], xs_s, xs_r, partner)
            cross.start()
            for to, value in rows_of(c):
                outv[block_at(c, BS), to : to + value.shape[1]] = value
            cross.wait()
            outv[block_at(1 - c, BS), :] = xin[0]
            out_copy(0, 256).start()
            out_copy(0, 256).wait()
            out_copy(256, 512).wait()

        end_level(at, False)

    def levels(uhi1, ulo1):
        def rest_of_one():
            g1.collect()
            split_update(0, uhi0, ulo0, 6, 8)

        def three():
            g3.collect()
            split_update(2, uhi1, ulo1, 0, 8)

        g1.send_pivot()
        g3.send()
        g3.send_pivot()
        level(0, uhi0, ulo0, rest_of_one, lambda: None)
        g3.share_out()
        level_two(three)
        level(2, uhi1, ulo1, lambda: None, lambda: split_update(3, uhi0, ulo0, 0, 8))
        level(3, uhi0, ulo0, lambda: None, lambda: None)

    pl.run_scoped(levels, pltpu.VMEM((ANC, SEP), BF16), pltpu.VMEM((ANC, SEP), BF16))
    for d in (2, 1, 3):
        for k in range(2):
            h_copy(k, d).wait_send()
    for k in range(2):

        @pl.when(jnp.logical_not(to_self(k)))
        def _():
            h_copy(k, 0).wait_send()

    g1.finish()
    g3.finish()
    for unit in range(4):
        u4_push(unit).wait_send()


def whole(blocks, root, updates, pivots):
    dma = pltpu.SemaphoreType.DMA
    any_space = pl.BlockSpec(memory_space=pl.ANY)
    smem = pl.BlockSpec(memory_space=pltpu.SMEM)
    gather_sems = []
    for n in (8, 2):
        gather_sems += [
            dma((2,)), dma((n,)), dma((n,)), dma((4, n)), dma((4, n)), dma((4,)), dma((4,)), dma((n,)), dma((n,)),
        ]
    outs = pl.pallas_call(
        whole_kernel,
        out_shape=[jax.ShapeDtypeStruct((1, 768, 1536), F32)]
        + [jax.ShapeDtypeStruct((2, 1024, 1024), F32)] * 2
        + [jax.ShapeDtypeStruct((1024, 1024), F32)],
        in_specs=[smem] * 4 + [any_space] * 9,
        out_specs=[any_space] * 4,
        scratch_shapes=[
            pltpu.VMEM((4, 4, BS, BS), F32),
            pltpu.VMEM((4, 4, BS, BS), F32),
            pltpu.VMEM((3, 4, BS, BS), F32),
            pltpu.VMEM((4, BS, BS), F32),
            pltpu.VMEM((2, 16, BS, BS), F32),
            pltpu.VMEM((4, 16, BS, BS), F32),
            pltpu.VMEM((4, 16, BS, BS), F32),
            pltpu.VMEM((4, BS, SEP), F32),
            pltpu.VMEM((4, BS, SEP), F32),
            pltpu.VMEM((16, BS, BS), F32),
            pltpu.VMEM((16, BS, BS), F32),
            pltpu.VMEM((2, 1024, 256), F32),
            pltpu.VMEM((ANC, 256), BF16),
            pltpu.VMEM((ANC, 256), BF16),
            pltpu.VMEM((ANC, SEP), BF16),
            pltpu.VMEM((ANC, SEP), BF16),
            pltpu.VMEM((2, UNIT, SEP), F32),
            pltpu.VMEM((512, ANC), BF16),
            pltpu.VMEM((8, 2, BS, BS), F32),
            pltpu.VMEM((2, BS, SEP), F32),
            pltpu.VMEM((2, BS, SEP), F32),
            pltpu.VMEM((BS, SEP), F32),
            pltpu.VMEM((2, BS, 1536), F32),
            pltpu.VMEM((768, 1536), F32),
            dma((16,)),
            dma,
            dma,
            dma((3,)),
            dma((3,)),
            dma((8,)),
            dma((8,)),
        ]
        + gather_sems
        + [
            dma((4,)),
            dma((4,)),
            dma,
            dma((2,)),
            dma,
            dma,
            dma((4, 2)),
            dma((4, 2)),
            dma((4,)),
            dma((4,)),
            dma((2,)),
            dma((8,)),
            dma((2, 8)),
            dma((8, 2)),
            dma((8, 2)),
            dma((2, 2)),
            dma((2, 2)),
            dma((2, 2)),
            dma((2, 2)),
            dma,
            dma,
            dma((2,)),
        ],
        compiler_params=pltpu.CompilerParams(
            collective_id=0, has_side_effects=True, vmem_limit_bytes=60 * 2**20
        ),
        name="whole",
    )(*blocks, root, *updates, *pivots)
    return outs[0]


def shards(
    root_inverse,
    blocks_one,
    blocks_two,
    blocks_three,
    blocks_four,
    update_one,
    update_two,
    update_three,
    update_four,
    pivot_one,
    pivot_two,
    pivot_three,
    pivot_four,
):
    return whole(
        (blocks_one, blocks_two, blocks_three, blocks_four),
        root_inverse.reshape(8, BS, 2048),
        (update_one, update_two, update_three, update_four),
        (pivot_one, pivot_two, pivot_three, pivot_four),
    )


def solution(mesh):
    mesh = Mesh(mesh.devices.reshape(2, 2, 2, 2, 4, 2), AXES)
    leaf = AXES[:4]
    placed = (
        P(leaf, ("row", "col")),
        P(),
        P(),
        P(),
        P(),
        P("col", leaf),
        P("col", leaf),
        P("col", leaf),
        P("col", leaf),
        P("row", leaf),
        P("row", leaf),
        P("row", leaf),
        P("row", leaf),
    )
    return jax.shard_map(
        shards, mesh=mesh, in_specs=placed, out_specs=P(leaf, "row", "col"), check_vma=False
    )
```
